128 devices in a mesh: row: 2 (over core), col: 2 (over x_lo), layer: 32 (over z, y, x_hi).
Axes of the slice: x: 4 (x_hi: 2, x_lo: 2; x = x_hi * 2 + x_lo), y: 4, z: 4, core: 2. Of those that a mesh axis runs over, the one named last changes fastest.
Arguments:
- left: bfloat16 [16384, 65536], P('row', ('layer', 'col'))
- pattern_left: int32 [64, 256], P('row', ('layer', 'col')), may hold values from 0 to 1, as said below
- right: bfloat16 [65536, 1024], P(('layer', 'row'), 'col'), may hold values from -0.0234375 to 0.0234375
- pattern_right: int32 [256, 4], P(('layer', 'row'), 'col'), may hold values from 0 to 1, as said below
- keep: int32 [64, 4], P(('row', 'layer'), 'col'), may hold values from 0 to 1, as said below
Outputs:
- flow: float32 [16384, 1024], P(('row', 'layer'), 'col')
The draws below stay inside these ranges and needn't reach their ends.
Inputs may be any that keep to these rules, and one draw needn't show every extreme that they name: `pattern_left`: column 0 of tiles is all ones; each tile row has its own share of stored tiles, from 0.2 to 0.8, and in each aligned block of 4 tile columns stores at most 3; tile row 0 stores exactly 3 in every block. `pattern_right`: row 0 of tiles is all ones; each tile column has its own share of stored tiles, from 0.2 to 0.8. `keep`: every tile column keeps the tile in tile row equal to its index modulo 16384 // 256.
All inputs are finite; a program needn't handle non-finite values.
Results may differ from the reference program's by a relative error of at most 0.0003.
Values may be sent and summed in bfloat16 or wider, within the bound.
A program may use at most 320 MiB of HBM per device.

```python
import jax
import jax.numpy as jnp
from jax import lax

TILE = 256
KI = 8
ROWS = 16384
INNER = 65536
COLS = 1024
N_COL = 2


def draw_left(key, part):
    key = jax.random.fold_in(key, 5)
    first, second = jax.random.split(key)
    rows = lax.broadcasted_iota(jnp.float32, (ROWS, 1), 0)
    rough = jnp.exp(jax.random.uniform(first, (ROWS, 1), jnp.float32, 0.0, 1.4))
    rising = jnp.exp(1.0986 * rows / ROWS)
    base = jax.random.normal(second, (ROWS, INNER), jnp.float32)
    return (base * rough * rising * 0.5).astype(jnp.bfloat16)


def draw_pattern_left(key, part):
    key = jax.random.fold_in(key, 11)
    first, second = jax.random.split(key)
    shape = (ROWS // TILE, INNER // TILE)
    level = jax.random.randint(first, (shape[0], 1), 20, 81)
    roll = jax.random.randint(second, shape, 0, 100)
    column = lax.broadcasted_iota(jnp.int32, shape, 1)
    row_index = lax.broadcasted_iota(jnp.int32, shape, 0)
    stored = jnp.where(column == 0, 1, (roll < level).astype(jnp.int32))
    stored = jnp.where(row_index == 0, 1, stored).astype(jnp.int32)
    width = KI // N_COL
    most = (3 * width + 3) // 4
    blocks = stored.reshape(shape[0], shape[1] // width, width)
    counted = jnp.cumsum(blocks, axis=2)
    capped = jnp.where(counted <= most, blocks, 0)
    return capped.reshape(shape).astype(jnp.int32)


def draw_pattern_right(key, part):
    key = jax.random.fold_in(key, 17)
    first, second = jax.random.split(key)
    shape = (INNER // TILE, COLS // TILE)
    level = jax.random.randint(first, (1, shape[1]), 20, 81)
    roll = jax.random.randint(second, shape, 0, 100)
    row_index = lax.broadcasted_iota(jnp.int32, shape, 0)
    return jnp.where(row_index == 0, 1, (roll < level).astype(jnp.int32)).astype(jnp.int32)


def draw_keep(key, part):
    key = jax.random.fold_in(key, 23)
    shape = (ROWS // TILE, COLS // TILE)
    roll = jax.random.randint(key, shape, 0, 100)
    row_index = lax.broadcasted_iota(jnp.int32, shape, 0)
    col_index = lax.broadcasted_iota(jnp.int32, shape, 1)
    forced = row_index == col_index % shape[0]
    return jnp.where(forced, 1, (roll < 75).astype(jnp.int32)).astype(jnp.int32)


def shard_levels(rng, dims, pieces, least, high):
    loudness = 1.0
    for dim, blocks in pieces:
        heights = jax.random.uniform(jax.random.fold_in(jax.random.fold_in(rng, 6), dim), (blocks,), jnp.float32, least / len(pieces), high / len(pieces))
        loudness = loudness * jnp.repeat(jnp.exp(heights), dims[dim] // blocks).reshape((-1,) + (1,) * (len(dims) - 1 - dim))
    return loudness


def gaussian(key, extent, deviation, limit, shards=(), kind=jnp.bfloat16):
    loudness = shard_levels(key, extent, shards, -0.22, 0.18) if shards else 1.0
    entries = jax.random.normal(key, extent, jnp.float32) * deviation * loudness
    return jnp.minimum(jnp.maximum(entries, -limit), limit).astype(kind)


def setup_inputs(seed: int = 0) -> dict:
    key_of = jax.random.split(jax.random.key(seed), 6)
    left = draw_left(jax.random.fold_in(key_of[5], 71), 0)
    pattern_left = draw_pattern_left(jax.random.fold_in(key_of[5], 71), 0)
    right = gaussian(key_of[2], (INNER, COLS), INNER ** -0.5, 0.0234375, ((0, 64), (1, 2)))
    pattern_right = draw_pattern_right(jax.random.fold_in(key_of[5], 71), 0)
    keep = draw_keep(jax.random.fold_in(key_of[5], 71), 0)
    return {"left": left, "pattern_left": pattern_left, "right": right, "pattern_right": pattern_right, "keep": keep}


def masked_tiles(values, pattern):
    rows, cols = values.shape
    tile_rows, tile_cols = pattern.shape
    shaped = values.reshape(tile_rows, rows // tile_rows, tile_cols, cols // tile_cols)
    return (shaped * pattern[:, None, :, None].astype(values.dtype)).reshape(rows, cols)


def reference(left, pattern_left, right, pattern_right, keep):
    left_kept = masked_tiles(left, pattern_left)
    right_kept = masked_tiles(right, pattern_right)
    expanded = jnp.dot(left_kept, right_kept, preferred_element_type=jnp.float32)
    inflated = masked_tiles(expanded * expanded, keep)
    totals = jnp.sum(inflated, axis=0)
    return jnp.float32(ROWS) * inflated / (totals + 1e-6)
```

```python
import functools
import math

import jax
import jax.numpy as jnp
from jax import lax
from jax.experimental import pallas as pl
from jax.experimental.pallas import tpu as pltpu
from jax.sharding import PartitionSpec as P

MESH = pl.DeviceIdType.MESH
TILE = 256
DEPTH = 1024
WIDE = 512
HEAD = 16
FINE = 64
TOP = 32700.0
A, B, C = 0, 1, 2
ROWS = (64, 96, 96)
START = (0, 64, 160)
PLAN = (
    ((2, 0), (2, 1), (0, 0), (3, 0), (1, 1), (0, 1), (1, 0), (3, 1)),
    ((2, 0), (3, 0), (0, 0), (2, 1), (1, 1), (0, 1), (1, 0), (3, 1)),
    ((2, 0), (3, 0), (0, 0), (2, 1), (1, 1), (0, 1), (1, 0), (3, 1)),
)
MESSAGES = (((2, 0), 1), ((2, 1), 3), ((3, 0), 3), ((1, 1), 1), ((1, 0), 1), ((3, 1), 3))
MERGED = {4: 0, 5: 1}
OWN = ((2, 4), (3, 5))
RING = ((0, 1, 2), (1, 2, 0), (2, 0, 1))


def place():
    layer = lax.axis_index("layer")
    x = lax.rem(layer, 2) * 2 + lax.axis_index("col")
    return lax.axis_index("row"), (x, lax.rem(layer // 2, 4), layer // 8)


def device(core, xyz):
    x, y, z = xyz
    return (core, lax.rem(x, 2), z * 8 + y * 2 + x // 2)


def moved(xyz, dim, by):
    return tuple(lax.rem(v + by, 4) if d == dim else v for d, v in enumerate(xyz))


def pick(table, index):
    value = jnp.int32(table[-1])
    for k in range(len(table) - 2, -1, -1):
        value = jnp.where(index == k, jnp.int32(table[k]), value)
    return value


def aligned(value, by=16):
    return pl.multiple_of(value, by)


def column_scale(codes):
    return jnp.exp(codes * (math.log(2.0) / FINE))


def encode(acc, segments, rows, out):
    top = jnp.zeros((HEAD, WIDE), jnp.float32)
    for base in segments:
        def look(i, top, base=base):
            return jnp.maximum(top, jnp.abs(acc[pl.ds(aligned(base + i * 16), 16), :]))

        top = lax.fori_loop(0, rows // 16, look, top)
    top = jnp.broadcast_to(jnp.max(top, axis=0, keepdims=True), (HEAD, WIDE))
    codes = jnp.ceil(jnp.log(jnp.maximum(top, 1e-30)) * (FINE / math.log(2.0)))
    out[pl.ds(0, HEAD), :] = codes.astype(jnp.int32).astype(jnp.int16)
    inverse = TOP / column_scale(codes)
    for k, base in enumerate(segments):
        def write(i, _, base=base, k=k):
            value = acc[pl.ds(aligned(base + i * 16), 16), :] * inverse
            out[pl.ds(aligned(HEAD + k * rows + i * 16), 16), :] = (
                jnp.round(value).astype(jnp.int32).astype(jnp.int16)
            )
            return 0

        lax.fori_loop(0, rows // 16, write, 0)


def add(acc, segments, rows, messages):
    scales = [
        column_scale(m[pl.ds(0, HEAD), :].astype(jnp.int32).astype(jnp.float32)) * (1.0 / TOP)
        for m in messages
    ]
    for k, base in enumerate(segments):
        def step(i, _, base=base, k=k):
            at = pl.ds(aligned(base + i * 16), 16)
            value = acc[at, :]
            for m, scale in zip(messages, scales):
                got = m[pl.ds(aligned(HEAD + k * rows + i * 16), 16), :]
                value += got.astype(jnp.int32).astype(jnp.float32) * scale
            acc[at, :] = value
            return 0

        lax.fori_loop(0, rows // 16, step, 0)


def kernel(
    left, pattern_left, right, pattern_right, keep, inflated, totals,
    panel, lefts, accs, send1, recv1, send2, recv2, send3, recv3, tsend, trecv,
    lsem, psend, precv, ssem1, rsem1, ssem2, rsem2, ssem3, rsem3, tssem, trsem,
):
    core, xyz = place()
    x, y, z = xyz
    col = lax.rem(x, 2)
    pair = (x + 1 - 2 * col, y, z)
    mate = device(1 - core, xyz)
    owner = core == col

    def load(part, step):
        by = pick([p[0] for p in PLAN[part]], step)
        half = pick([p[1] for p in PLAN[part]], step)
        rows = pl.ds(START[part], ROWS[part])
        if part == A:
            source = left.at[pl.ds(half * 2, 2), :, lax.rem(x + by, 4) // 2, rows, :]
        elif part == B:
            source = left.at[:, lax.rem(y + by, 4), :, rows, :]
        else:
            source = left.at[lax.rem(z + by, 4), :, :, rows, :]
        return pltpu.make_async_copy(source, lefts[part], lsem.at[part])

    for part in (B, C, A):
        load(part, jnp.int32(0)).start()

    peers = [mate, device(1 - core, pair), device(1 - core, moved(xyz, 0, 2))]
    peers += [device(core, moved(xyz, d, by)) for d in range(3) for by in (1, 2, 3)]
    barrier = pltpu.get_barrier_semaphore()
    for peer in peers:
        pl.semaphore_signal(barrier, inc=1, device_id=peer, device_id_type=MESH)

    slot = jnp.where(owner, 0, 2)
    for k in range(4):
        for j in range(2):
            at = (pl.ds(k * TILE, TILE), pl.ds(j * TILE, TILE))
            mask = jnp.full((TILE, TILE), pattern_right[k, j].astype(jnp.float32))
            panel[(slot,) + at] = right[at] * mask.astype(jnp.bfloat16)
    pl.semaphore_wait(barrier, len(peers))

    HALF = DEPTH // 2

    def share():
        return pltpu.make_async_remote_copy(
            panel.at[0], panel.at[0], psend.at[0], precv.at[0], device_id=mate, device_id_type=MESH
        )

    def export(to):
        rows = pl.ds(to * HALF, HALF)
        return pltpu.make_async_remote_copy(
            panel.at[2, rows], panel.at[1, rows], psend.at[1 + to], precv.at[1],
            device_id=device(jnp.int32(to), pair), device_id_type=MESH,
        )

    def forward():
        rows = pl.ds(aligned(core * HALF), HALF)
        return pltpu.make_async_remote_copy(
            panel.at[1, rows], panel.at[1, rows], psend.at[3], precv.at[2], device_id=mate, device_id_type=MESH
        )

    @pl.when(owner)
    def _():
        share().start()

    @pl.when(jnp.logical_not(owner))
    def _():
        export(0).start()
        export(1).start()
        share().wait_recv()

    def message1(part, k):
        to = device(core, moved(xyz, RING[part][0], MESSAGES[k][1]))
        return pltpu.make_async_remote_copy(
            send1[part].at[k], recv1[part].at[k], ssem1.at[part, k], rsem1.at[part, k],
            device_id=to, device_id_type=MESH,
        )

    def multiply(part, step):
        by = pick([p[0] for p in PLAN[part]], step)
        half = pick([p[1] for p in PLAN[part]], step)
        rows = ROWS[part]
        load(part, step).wait()
        block = lefts[part]
        for a in range(block.shape[0]):
            for b in range(block.shape[1]):
                if part == A:
                    tile = (half * 2 + a) * 8 + b * 2 + lax.rem(x + by, 4) // 2
                elif part == B:
                    tile = a * 8 + lax.rem(y + by, 4) * 2 + b
                else:
                    tile = lax.rem(z + by, 4) * 8 + a * 2 + b
                for k in range(4):
                    at = (a, b, slice(None), pl.ds(k * TILE, TILE))
                    mask = jnp.full((rows, TILE), pattern_left[tile, k].astype(jnp.float32))
                    block[at] = block[at] * mask.astype(jnp.bfloat16)
        columns = lax.rem(by, 2) if part == A else half
        to = jnp.where(by == 0, half, 2)
        accs[part][pl.ds(aligned(to * (8 * rows)), 8 * rows), :] = jnp.dot(
            block[...].reshape(8 * rows, DEPTH), panel[columns], preferred_element_type=jnp.float32
        )

        @pl.when(step < 7)
        def _():
            load(part, step + 1).start()

    def steps(step, _):
        @pl.when(step == 3)
        def _():
            export(0).wait_recv()
            forward().start()
            forward().wait_recv()
            for k in (0, 1):
                message1(A, k).start()

        for part in (B, C, A):
            rows = 8 * ROWS[part]
            multiply(part, step)
            for k, merged in MERGED.items():
                @pl.when(step == PLAN[part].index(MESSAGES[k][0]))
                def _(k=k, merged=merged, part=part, rows=rows):
                    message1(part, merged).wait_recv()
                    add(accs[part], [2 * rows], rows, [recv1[part].at[merged]])

            at = [PLAN[part].index(m[0]) for m in MESSAGES]
            sends = functools.reduce(jnp.logical_or, [step == i for i in at])

            @pl.when(sends)
            def _(part=part, rows=rows, at=at):
                k = sum(jnp.where(step == i, n, 0) for n, i in enumerate(at))
                encode(accs[part], [2 * rows], rows, send1[part].at[k])

            for k, i in enumerate(at):
                if part != A or k > 1:
                    @pl.when(step == i)
                    def _(k=k, part=part):
                        message1(part, k).start()

        return 0

    lax.fori_loop(0, 8, steps, 0)

    def bases2(part, by, half):
        rows = ROWS[part]
        if part == A:
            return [half * (8 * rows) + (a * 4 + lax.rem(y + by, 4)) * rows for a in (0, 1)]
        if part == B:
            return [half * (8 * rows) + (lax.rem(z + by, 4) * 2 + b) * rows for b in (0, 1)]
        return [(by % 2) * (8 * rows) + ((half * 2 + a) * 2 + lax.rem(x + by, 4) // 2) * rows for a in (0, 1)]

    def message2(part, k):
        to = device(core, moved(xyz, RING[part][1], MESSAGES[k][1]))
        return pltpu.make_async_remote_copy(
            send2[part].at[k], recv2[part].at[k], ssem2.at[part, k], rsem2.at[part, k],
            device_id=to, device_id_type=MESH,
        )

    for part in (B, C, A):
        rows = 8 * ROWS[part]
        for half in (0, 1):
            for k in OWN[half]:
                message1(part, k).wait_recv()
            add(accs[part], [half * rows], rows, [recv1[part].at[k] for k in OWN[half]])
        for k in (0, 1, 2, 3):
            encode(accs[part], bases2(part, *MESSAGES[k][0]), ROWS[part], send2[part].at[k])
            message2(part, k).start()
    for part in (B, C, A):
        for k, merged in MERGED.items():
            bases = bases2(part, *MESSAGES[k][0])
            message2(part, merged).wait_recv()
            add(accs[part], bases, ROWS[part], [recv2[part].at[merged]])
            encode(accs[part], bases, ROWS[part], send2[part].at[k])
            message2(part, k).start()

    def base3(part, by):
        rows = ROWS[part]
        if part == A:
            to = lax.rem(z + by, 4)
            return to // 2 * (8 * rows) + (lax.rem(to, 2) * 4 + y) * rows
        if part == B:
            return (by % 2) * (8 * rows) + (z * 2 + lax.rem(x + by, 4) // 2) * rows
        return (lax.rem(y + by, 4) * 2 + x // 2) * rows

    def message3(part, by):
        to = device(core, moved(xyz, RING[part][2], by))
        return pltpu.make_async_remote_copy(
            send3[part].at[by - 1], recv3[part].at[by - 1], ssem3.at[part, by - 1], rsem3.at[part, by - 1],
            device_id=to, device_id_type=MESH,
        )

    for part in (B, C, A):
        for half in (0, 1):
            for k in OWN[half]:
                message2(part, k).wait_recv()
            add(accs[part], bases2(part, 0, half), ROWS[part], [recv2[part].at[k] for k in OWN[half]])
        for by in (2, 1, 3):
            encode(accs[part], [base3(part, by)], ROWS[part], send3[part].at[by - 1])
            message3(part, by).start()

    keeps = [keep[0, j].astype(jnp.float32) for j in range(2)]
    sums = jnp.zeros((16, WIDE), jnp.float32)
    for part in (B, C, A):
        for by in (2, 1, 3):
            message3(part, by).wait_recv()
        add(accs[part], [base3(part, 0)], ROWS[part], [recv3[part].at[by - 1] for by in (2, 1, 3)])
        kept = jnp.concatenate([jnp.full((16, TILE), v) for v in keeps], axis=1)

        def finish(i, sums, part=part, kept=kept):
            value = accs[part][pl.ds(aligned(base3(part, 0) + i * 16), 16), :]
            value = value * value * kept
            inflated[pl.ds(aligned(START[part] + i * 16), 16), :] = value
            return sums + value

        sums = lax.fori_loop(0, ROWS[part] // 16, finish, sums)
    sums = jnp.sum(sums, axis=0, keepdims=True)

    rounds = (
        [mate, device(core, moved(xyz, 0, 2)), device(1 - core, moved(xyz, 0, 2))],
        [device(core, moved(xyz, 1, by)) for by in (1, 2, 3)],
        [device(core, moved(xyz, 2, by)) for by in (1, 2, 3)],
    )
    total = jnp.concatenate([sums[:, k * 128 : (k + 1) * 128] for k in range(4)] + [jnp.zeros((4, 128), jnp.float32)], axis=0)
    copies = []
    for n, group in enumerate(rounds):
        tsend[n] = total
        now = [
            pltpu.make_async_remote_copy(
                tsend.at[n], trecv.at[n, k], tssem.at[n, k], trsem.at[n, k], device_id=peer, device_id_type=MESH
            )
            for k, peer in enumerate(group)
        ]
        for copy in now:
            copy.start()
        for k, copy in enumerate(now):
            copy.wait_recv()
            total = total + trecv[n, k]
        copies += now
    totals[...] = total

    for copy in copies:
        copy.wait_send()
    for part in range(3):
        for k in range(6):
            message1(part, k).wait_send()
            message2(part, k).wait_send()
        for by in (1, 2, 3):
            message3(part, by).wait_send()
    forward().wait_send()

    @pl.when(owner)
    def _():
        share().wait_send()

    @pl.when(jnp.logical_not(owner))
    def _():
        export(0).wait_send()
        export(1).wait_send()


def body(left, pattern_left, right, pattern_right, keep):
    vmem = pl.BlockSpec(memory_space=pltpu.VMEM)
    smem = pl.BlockSpec(memory_space=pltpu.SMEM)
    dma = pltpu.SemaphoreType.DMA
    blocks = [(2, 4), (4, 2), (4, 2)]
    inflated, totals = pl.pallas_call(
        kernel,
        out_shape=(jax.ShapeDtypeStruct((TILE, WIDE), jnp.float32), jax.ShapeDtypeStruct((8, 128), jnp.float32)),
        in_specs=[pl.BlockSpec(memory_space=pl.ANY), smem, vmem, smem, smem],
        out_specs=(vmem, vmem),
        scratch_shapes=[
            pltpu.VMEM((3, DEPTH, WIDE), jnp.bfloat16),
            [pltpu.VMEM(b + (r, DEPTH), jnp.bfloat16) for b, r in zip(blocks, ROWS)],
            [pltpu.VMEM((3 * 8 * r, WIDE), jnp.float32) for r in ROWS],
            [pltpu.VMEM((6, HEAD + 8 * r, WIDE), jnp.int16) for r in ROWS],
            [pltpu.VMEM((6, HEAD + 8 * r, WIDE), jnp.int16) for r in ROWS],
            [pltpu.VMEM((6, HEAD + 2 * r, WIDE), jnp.int16) for r in ROWS],
            [pltpu.VMEM((6, HEAD + 2 * r, WIDE), jnp.int16) for r in ROWS],
            [pltpu.VMEM((3, HEAD + r, WIDE), jnp.int16) for r in ROWS],
            [pltpu.VMEM((3, HEAD + r, WIDE), jnp.int16) for r in ROWS],
            pltpu.VMEM((3, 8, 128), jnp.float32),
            pltpu.VMEM((3, 3, 8, 128), jnp.float32),
            dma((3,)), dma((4,)), dma((3,)), dma((3, 6)), dma((3, 6)), dma((3, 6)), dma((3, 6)),
            dma((3, 3)), dma((3, 3)), dma((3, 3)), dma((3, 3)),
        ],
        compiler_params=pltpu.CompilerParams(
            collective_id=0, has_side_effects=True, vmem_limit_bytes=62 * 1024 * 1024
        ),
        name="expand",
    )(left.reshape(4, 4, 2, TILE, DEPTH), pattern_left, right, pattern_right, keep)
    return jnp.float32(16384) * inflated / (totals[:4].reshape(WIDE) + 1e-6)


def solution(mesh):
    return jax.shard_map(
        body,
        mesh=mesh,
        in_specs=(
            P("row", ("layer", "col")),
            P("row", ("layer", "col")),
            P(("layer", "row"), "col"),
            P(("layer", "row"), "col"),
            P(("row", "layer"), "col"),
        ),
        out_specs=P(("row", "layer"), "col"),
        check_vma=False,
    )
```

```python
import functools
import math

import jax
import jax.numpy as jnp
from jax import lax
from jax.experimental import pallas as pl
from jax.experimental.pallas import tpu as pltpu
from jax.sharding import PartitionSpec as P

MESH = pl.DeviceIdType.MESH
TILE = 256
DEPTH = 1024
WIDE = 512
LANES = 128
GROUPS = WIDE // LANES
HEAD = 16
FINE = 64
TOP = 32700.0
A, B, C = 0, 1, 2
ORDER = (B, C, A)
SUBS = 2
ROWS = (32, 48, 48)
START = (0, 64, 160)
PLAN = (
    ((2, 0), (2, 1), (0, 0), (3, 0), (1, 1), (0, 1), (1, 0), (3, 1)),
    ((2, 0), (3, 0), (0, 0), (2, 1), (1, 1), (0, 1), (1, 0), (3, 1)),
    ((2, 0), (3, 0), (0, 0), (2, 1), (1, 1), (0, 1), (1, 0), (3, 1)),
)
STEPS = len(PLAN[0])
MESSAGES = (((2, 0), 1), ((2, 1), 3), ((3, 0), 3), ((1, 1), 1), ((1, 0), 1), ((3, 1), 3))
MERGED = {4: 0, 5: 1}
OWN = ((2, 4), (3, 5))
RING = ((0, 1, 2), (1, 2, 0), (2, 0, 1))


def place():
    layer = lax.axis_index("layer")
    x = lax.rem(layer, 2) * 2 + lax.axis_index("col")
    return lax.axis_index("row"), (x, lax.rem(layer // 2, 4), layer // 8)


def device(core, xyz):
    x, y, z = xyz
    return (core, lax.rem(x, 2), z * 8 + y * 2 + x // 2)


def moved(xyz, dim, by):
    return tuple(lax.rem(v + by, 4) if d == dim else v for d, v in enumerate(xyz))


def pick(table, index):
    value = jnp.int32(table[-1])
    for k in range(len(table) - 2, -1, -1):
        value = jnp.where(index == k, jnp.int32(table[k]), value)
    return value


def aligned(value, by=16):
    return pl.multiple_of(value, by)


def loop(count, step, init):
    return lax.fori_loop(0, count, step, init, unroll=True if count <= 6 else 4)


def column_scale(codes):
    return jnp.exp(codes * (math.log(2.0) / FINE))


def encode(acc, segments, rows, out):
    top = jnp.zeros((HEAD, WIDE), jnp.float32)
    for base in segments:
        def look(i, top, base=base):
            return jnp.maximum(top, jnp.abs(acc[pl.ds(aligned(base + i * 16), 16), :]))

        top = loop(rows // 16, look, top)
    top = jnp.broadcast_to(jnp.max(top, axis=0, keepdims=True), (HEAD, WIDE))
    codes = jnp.ceil(jnp.log(jnp.maximum(top, 1e-30)) * (FINE / math.log(2.0)))
    row = lax.broadcasted_iota(jnp.int32, (HEAD, LANES), 0)
    head = codes[:, :LANES]
    for g in range(1, GROUPS):
        head = jnp.where(row == g, codes[:, g * LANES : (g + 1) * LANES], head)
    out[pl.ds(0, HEAD), :] = head.astype(jnp.int32).astype(jnp.int16)
    inverse = TOP / column_scale(codes)
    for k, base in enumerate(segments):
        def write(i, _, base=base, k=k):
            value = jnp.round(acc[pl.ds(aligned(base + i * 16), 16), :] * inverse)
            value = value.astype(jnp.int32).astype(jnp.int16)
            for g in range(GROUPS):
                at = HEAD + (g * len(segments) + k) * rows + i * 16
                out[pl.ds(aligned(at), 16), :] = value[:, g * LANES : (g + 1) * LANES]
            return 0

        loop(rows // 16, write, 0)


def add(acc, segments, rows, messages):
    scales = []
    for m in messages:
        head = column_scale(m[pl.ds(0, HEAD), :].astype(jnp.int32).astype(jnp.float32)) * (1.0 / TOP)
        scales.append([jnp.broadcast_to(head[g : g + 1, :], (16, LANES)) for g in range(GROUPS)])
    for k, base in enumerate(segments):
        def step(i, _, base=base, k=k):
            at = pl.ds(aligned(base + i * 16), 16)
            for g in range(GROUPS):
                lanes = pl.ds(g * LANES, LANES)
                value = acc[at, lanes]
                for m, scale in zip(messages, scales):
                    got = m[pl.ds(aligned(HEAD + (g * len(segments) + k) * rows + i * 16), 16), :]
                    value += got.astype(jnp.int32).astype(jnp.float32) * scale[g]
                acc[at, lanes] = value
            return 0

        loop(rows // 16, step, 0)


def kernel(
    left, pattern_left, right, pattern_right, keep, inflated, totals,
    panel, lefts, accs, send1, recv1, send2, recv2, send3, recv3, tsend, trecv,
    lsem, psem, psend, precv, ssem1, rsem1, ssem2, rsem2, ssem3, rsem3, tssem, trsem,
):
    core, xyz = place()
    x, y, z = xyz
    col = lax.rem(x, 2)
    pair = (x + 1 - 2 * col, y, z)
    mate = device(1 - core, xyz)
    owner = core == col
    slot = jnp.where(owner, 0, 2)
    fetch = pltpu.make_async_copy(right, panel.at[slot], psem)
    fetch.start()

    def load(part, step):
        sub, step = step // STEPS, lax.rem(step, STEPS)
        by = pick([p[0] for p in PLAN[part]], step)
        half = pick([p[1] for p in PLAN[part]], step)
        rows = pl.ds(aligned(START[part] + sub * ROWS[part]), ROWS[part])
        if part == A:
            source = left.at[pl.ds(half * 2, 2), :, lax.rem(x + by, 4) // 2, rows, :]
        elif part == B:
            source = left.at[:, lax.rem(y + by, 4), :, rows, :]
        else:
            source = left.at[lax.rem(z + by, 4), :, :, rows, :]
        return pltpu.make_async_copy(source, lefts[part], lsem.at[part])

    for part in ORDER:
        load(part, jnp.int32(0)).start()

    rounds = (
        [mate] + [device(c, moved(xyz, 1, by)) for by in (1, 2, 3) for c in (core, 1 - core)],
        [device(core, moved(xyz, 0, 2))]
        + [device(core, moved(moved(xyz, 2, by), 0, dx)) for by in (1, 2, 3) for dx in (0, 2)],
    )
    peers = [p for group in rounds for p in group]
    peers += [device(1 - core, pair), device(core, moved(xyz, 0, 1)), device(core, moved(xyz, 0, 3))]
    barrier = pltpu.get_barrier_semaphore()
    for peer in peers:
        pl.semaphore_signal(barrier, inc=1, device_id=peer, device_id_type=MESH)

    fetch.wait()
    for k in range(4):
        for j in range(2):
            at = (slot, pl.ds(k * TILE, TILE), pl.ds(j * TILE, TILE))
            mask = jnp.full((TILE, TILE), pattern_right[j, k].astype(jnp.float32))
            panel[at] = panel[at] * mask.astype(jnp.bfloat16)
    pl.semaphore_wait(barrier, len(peers))

    HALF = DEPTH // 2

    def share():
        return pltpu.make_async_remote_copy(
            panel.at[0], panel.at[0], psend.at[0], precv.at[0], device_id=mate, device_id_type=MESH
        )

    def export(to):
        rows = pl.ds(to * HALF, HALF)
        return pltpu.make_async_remote_copy(
            panel.at[2, rows], panel.at[1, rows], psend.at[1 + to], precv.at[1],
            device_id=device(jnp.int32(to), pair), device_id_type=MESH,
        )

    def forward():
        rows = pl.ds(aligned(core * HALF), HALF)
        return pltpu.make_async_remote_copy(
            panel.at[1, rows], panel.at[1, rows], psend.at[3], precv.at[2], device_id=mate, device_id_type=MESH
        )

    @pl.when(owner)
    def _():
        share().start()

    @pl.when(jnp.logical_not(owner))
    def _():
        export(0).start()
        export(1).start()
        share().wait_recv()

    def message(ring, part, sub, k):
        send, recv, ssem, rsem = (
            (send1, recv1, ssem1, rsem1),
            (send2, recv2, ssem2, rsem2),
            (send3, recv3, ssem3, rsem3),
        )[ring]
        count, by = (3, k + 1) if ring == 2 else (6, MESSAGES[k][1])
        n = sub * count + k
        return pltpu.make_async_remote_copy(
            send[part].at[n], recv[part].at[n], ssem.at[part, n], rsem.at[part, n],
            device_id=device(core, moved(xyz, RING[part][ring], by)), device_id_type=MESH,
        )

    def base1(part, sub, half):
        return (sub * 2 + half) * (8 * ROWS[part])

    WORK = SUBS * 2 * 8

    def multiply(part, step, sub, i):
        by = pick([p[0] for p in PLAN[part]], i)
        half = pick([p[1] for p in PLAN[part]], i)
        rows = ROWS[part]
        load(part, step).wait()
        block = lefts[part]
        for a in range(block.shape[0]):
            for b in range(block.shape[1]):
                if part == A:
                    tile = (half * 2 + a) * 8 + b * 2 + lax.rem(x + by, 4) // 2
                elif part == B:
                    tile = a * 8 + lax.rem(y + by, 4) * 2 + b
                else:
                    tile = lax.rem(z + by, 4) * 8 + a * 2 + b
                for k in range(4):
                    at = (a, b, slice(None), pl.ds(k * TILE, TILE))
                    mask = jnp.full((rows, TILE), pattern_left[k, tile].astype(jnp.float32))
                    block[at] = block[at] * mask.astype(jnp.bfloat16)
        columns = lax.rem(by, 2) if part == A else half
        to = jnp.where(by == 0, base1(part, sub, half), WORK * rows)
        accs[part][pl.ds(aligned(to), 8 * rows), :] = jnp.dot(
            block[...].reshape(8 * rows, DEPTH), panel[columns], preferred_element_type=jnp.float32
        )

        @pl.when(step < SUBS * STEPS - 1)
        def _():
            load(part, step + 1).start()

    def bases2(part, sub, by, half):
        rows = ROWS[part]
        if part == A:
            return [base1(part, sub, half) + (a * 4 + lax.rem(y + by, 4)) * rows for a in (0, 1)]
        if part == B:
            return [base1(part, sub, half) + (lax.rem(z + by, 4) * 2 + b) * rows for b in (0, 1)]
        at = [(half * 2 + a) * 2 + lax.rem(x + by, 4) // 2 for a in (0, 1)]
        return [base1(part, sub, by % 2) + a * rows for a in at]

    def base3(part, sub, by):
        rows = ROWS[part]
        if part == A:
            to = lax.rem(z + by, 4)
            return base1(part, sub, to // 2) + (lax.rem(to, 2) * 4 + y) * rows
        if part == B:
            return base1(part, sub, by % 2) + (z * 2 + lax.rem(x + by, 4) // 2) * rows
        return base1(part, sub, 0) + (lax.rem(y + by, 4) * 2 + x // 2) * rows

    def second_first(sub):
        for part in ORDER:
            for half in (0, 1):
                for k in OWN[half]:
                    message(0, part, sub, k).wait_recv()
                got = [recv1[part].at[sub * 6 + k] for k in OWN[half]]
                add(accs[part], [base1(part, sub, half)], 8 * ROWS[part], got)
            for k in (0, 1, 2, 3):
                encode(accs[part], bases2(part, sub, *MESSAGES[k][0]), ROWS[part], send2[part].at[sub * 6 + k])
                message(1, part, sub, k).start()

    def second_merge(sub):
        for part in ORDER:
            for k, merged in MERGED.items():
                bases = bases2(part, sub, *MESSAGES[k][0])
                message(1, part, sub, merged).wait_recv()
                add(accs[part], bases, ROWS[part], [recv2[part].at[sub * 6 + merged]])
                encode(accs[part], bases, ROWS[part], send2[part].at[sub * 6 + k])
                message(1, part, sub, k).start()

    def third(sub):
        for part in ORDER:
            for half in (0, 1):
                for k in OWN[half]:
                    message(1, part, sub, k).wait_recv()
                got = [recv2[part].at[sub * 6 + k] for k in OWN[half]]
                add(accs[part], bases2(part, sub, 0, half), ROWS[part], got)
            for by in (2, 1, 3):
                encode(accs[part], [base3(part, sub, by)], ROWS[part], send3[part].at[sub * 3 + by - 1])
                message(2, part, sub, by - 1).start()

    keeps = [keep[0, j].astype(jnp.float32) for j in range(2)]
    kept = jnp.concatenate([jnp.full((16, TILE), v) for v in keeps], axis=1)

    def finish(sub, sums):
        for part in ORDER:
            for by in (2, 1, 3):
                message(2, part, sub, by - 1).wait_recv()
            base = base3(part, sub, 0)
            add(accs[part], [base], ROWS[part], [recv3[part].at[sub * 3 + by - 1] for by in (2, 1, 3)])
            for i in range(ROWS[part] // 16):
                value = accs[part][pl.ds(aligned(base + i * 16), 16), :]
                value = value * value * kept
                inflated[pl.ds(START[part] + sub * ROWS[part] + i * 16, 16), :] = value
                sums = sums + value
        return sums

    def steps(step, _):
        sub, i = step // STEPS, lax.rem(step, STEPS)

        @pl.when(step == 3)
        def _():
            export(0).wait_recv()
            forward().start()
            forward().wait_recv()
            for k in (0, 1):
                message(0, A, 0, k).start()

        @pl.when(step == STEPS + 6)
        def _():
            second_first(0)

        for part in ORDER:
            rows = 8 * ROWS[part]
            work = WORK * ROWS[part]
            multiply(part, step, sub, i)
            for k, merged in MERGED.items():
                @pl.when(i == PLAN[part].index(MESSAGES[k][0]))
                def _(merged=merged, part=part, rows=rows, work=work):
                    message(0, part, sub, merged).wait_recv()
                    add(accs[part], [work], rows, [recv1[part].at[sub * 6 + merged]])

            at = [PLAN[part].index(m[0]) for m in MESSAGES]

            @pl.when(functools.reduce(jnp.logical_or, [i == j for j in at]))
            def _(part=part, rows=rows, at=at, work=work):
                k = sum(jnp.where(i == j, n, 0) for n, j in enumerate(at))
                encode(accs[part], [work], rows, send1[part].at[sub * 6 + k])

            for k, j in enumerate(at):
                now = i == j
                if part == A and k < 2:
                    now = jnp.logical_and(now, sub > 0)

                @pl.when(now)
                def _(k=k, part=part):
                    message(0, part, sub, k).start()

        return 0

    lax.fori_loop(0, SUBS * STEPS, steps, 0)
    sums = jnp.zeros((16, WIDE), jnp.float32)
    second_merge(0)
    second_first(1)
    third(0)
    second_merge(1)
    sums = finish(0, sums)
    third(1)
    sums = finish(1, sums)
    sums = jnp.sum(sums, axis=0, keepdims=True)

    parts = [sums[:, g * LANES : (g + 1) * LANES] for g in range(GROUPS)]
    total = jnp.concatenate(parts + [jnp.zeros((8 - GROUPS, LANES), jnp.float32)], axis=0)
    copies = []
    for n, group in enumerate(rounds):
        tsend[n] = total
        now = [
            pltpu.make_async_remote_copy(
                tsend.at[n], trecv.at[n, k], tssem.at[n, k], trsem.at[n, k], device_id=peer, device_id_type=MESH
            )
            for k, peer in enumerate(group)
        ]
        for copy in now:
            copy.start()
        for k, copy in enumerate(now):
            copy.wait_recv()
            total = total + trecv[n, k]
        copies += now
    for g in range(GROUPS):
        totals[:, pl.ds(g * LANES, LANES)] = total[g : g + 1, :] + 1e-6

    for copy in copies:
        copy.wait_send()
    for part in range(3):
        for sub in range(SUBS):
            for k in range(6):
                message(0, part, sub, k).wait_send()
                message(1, part, sub, k).wait_send()
            for k in range(3):
                message(2, part, sub, k).wait_send()
    forward().wait_send()

    @pl.when(owner)
    def _():
        share().wait_send()

    @pl.when(jnp.logical_not(owner))
    def _():
        export(0).wait_send()
        export(1).wait_send()


def body(left, pattern_left, right, pattern_right, keep):
    vmem = pl.BlockSpec(memory_space=pltpu.VMEM)
    smem = pl.BlockSpec(memory_space=pltpu.SMEM)
    hbm = pl.BlockSpec(memory_space=pl.ANY)
    dma = pltpu.SemaphoreType.DMA
    blocks = [(2, 4), (4, 2), (4, 2)]

    def buffers(count, pieces):
        return [
            pltpu.VMEM((SUBS * count, HEAD + GROUPS * pieces * r, LANES), jnp.int16) for r in ROWS
        ]

    inflated, totals = pl.pallas_call(
        kernel,
        out_shape=(jax.ShapeDtypeStruct((TILE, WIDE), jnp.float32), jax.ShapeDtypeStruct((1, WIDE), jnp.float32)),
        in_specs=[hbm, smem, hbm, smem, smem],
        out_specs=(vmem, vmem),
        scratch_shapes=[
            pltpu.VMEM((3, DEPTH, WIDE), jnp.bfloat16),
            [pltpu.VMEM(b + (r, DEPTH), jnp.bfloat16) for b, r in zip(blocks, ROWS)],
            [pltpu.VMEM(((SUBS * 2 + 1) * 8 * r, WIDE), jnp.float32) for r in ROWS],
            buffers(6, 8), buffers(6, 8), buffers(6, 2), buffers(6, 2), buffers(3, 1), buffers(3, 1),
            pltpu.VMEM((2, 8, LANES), jnp.float32),
            pltpu.VMEM((2, 7, 8, LANES), jnp.float32),
            dma((3,)), dma, dma((4,)), dma((3,)), dma((3, SUBS * 6)), dma((3, SUBS * 6)),
            dma((3, SUBS * 6)), dma((3, SUBS * 6)), dma((3, SUBS * 3)), dma((3, SUBS * 3)), dma((2, 7)), dma((2, 7)),
        ],
        compiler_params=pltpu.CompilerParams(
            collective_id=0, has_side_effects=True, vmem_limit_bytes=60 * 1024 * 1024
        ),
        name="expand",
    )(left.reshape(4, 4, 2, TILE, DEPTH), pattern_left.T, right, pattern_right.T, keep)
    return jnp.float32(16384) * inflated / totals


def solution(mesh):
    return jax.shard_map(
        body,
        mesh=mesh,
        in_specs=(
            P("row", ("layer", "col")),
            P("row", ("layer", "col")),
            P(("layer", "row"), "col"),
            P(("layer", "row"), "col"),
            P(("row", "layer"), "col"),
        ),
        out_specs=P(("row", "layer"), "col"),
        check_vma=False,
    )
```

```python
import math

import jax
import jax.numpy as jnp
from jax import lax
from jax.experimental import pallas as pl
from jax.experimental.pallas import tpu as pltpu
from jax.sharding import PartitionSpec as P

MESH = pl.DeviceIdType.MESH
TILE = 256
DEPTH = 1024
WIDE = 512
LANES = 128
GROUPS = WIDE // LANES
HEAD = 16
FINE = 64
TOP = 32700.0
A, B, C = 0, 1, 2
ORDER = (B, C, A)
SUBS = 2
ROWS = (32, 48, 48)
START = (0, 64, 160)
PLAN_A = (
    (0, 2, 0), (0, 2, 1), (1, 2, 0), (1, 2, 1), (0, 0, 0), (1, 0, 0), (0, 0, 1), (0, 3, 0),
    (0, 1, 1), (0, 1, 0), (0, 3, 1), (1, 3, 0), (1, 1, 1), (1, 1, 0), (1, 3, 1), (1, 0, 1),
)
PLAN_BC = (
    (0, 2, 0), (0, 3, 0), (1, 2, 0), (1, 3, 0), (0, 0, 0), (1, 0, 0), (0, 1, 0), (0, 2, 1),
    (1, 2, 1), (0, 1, 1), (1, 1, 1), (1, 1, 0), (0, 0, 1), (0, 3, 1), (1, 0, 1), (1, 3, 1),
)
PLAN = (PLAN_A, PLAN_BC, PLAN_BC)
STEPS = len(PLAN_A)
EARLY, WHOLE = 5, 7
MESSAGES = (((2, 0), 1), ((2, 1), 3), ((3, 0), 3), ((1, 1), 1), ((1, 0), 1), ((3, 1), 3))
MERGED = {4: 0, 5: 1}
OWN = ((2, 4), (3, 5))
RING = ((0, 1, 2), (1, 2, 0), (2, 0, 1))


def place():
    layer = lax.axis_index("layer")
    x = lax.rem(layer, 2) * 2 + lax.axis_index("col")
    return lax.axis_index("row"), (x, lax.rem(layer // 2, 4), layer // 8)


def device(core, xyz):
    x, y, z = xyz
    return (core, lax.rem(x, 2), z * 8 + y * 2 + x // 2)


def moved(xyz, dim, by):
    return tuple(lax.rem(v + by, 4) if d == dim else v for d, v in enumerate(xyz))


def pick(table, index):
    value = jnp.int32(table[-1])
    for k in range(len(table) - 2, -1, -1):
        value = jnp.where(index == k, jnp.int32(table[k]), value)
    return value


def aligned(value, by=16):
    return pl.multiple_of(value, by)


def loop(count, step, init):
    return lax.fori_loop(0, count, step, init, unroll=True if count <= 6 else 4)


def column_scale(codes):
    return jnp.exp(codes * (math.log(2.0) / FINE))


def encode(acc, segments, rows, out):
    top = jnp.zeros((HEAD, WIDE), jnp.float32)
    for base in segments:
        def look(i, top, base=base):
            return jnp.maximum(top, jnp.abs(acc[pl.ds(aligned(base + i * 16), 16), :]))

        top = loop(rows // 16, look, top)
    top = jnp.broadcast_to(jnp.max(top, axis=0, keepdims=True), (HEAD, WIDE))
    codes = jnp.ceil(jnp.log(jnp.maximum(top, 1e-30)) * (FINE / math.log(2.0)))
    row = lax.broadcasted_iota(jnp.int32, (HEAD, LANES), 0)
    head = codes[:, :LANES]
    for g in range(1, GROUPS):
        head = jnp.where(row == g, codes[:, g * LANES : (g + 1) * LANES], head)
    out[pl.ds(0, HEAD), :] = head.astype(jnp.int32).astype(jnp.int16)
    inverse = TOP / column_scale(codes)
    for k, base in enumerate(segments):
        def write(i, _, base=base, k=k):
            value = jnp.round(acc[pl.ds(aligned(base + i * 16), 16), :] * inverse)
            value = value.astype(jnp.int32).astype(jnp.int16)
            for g in range(GROUPS):
                at = HEAD + (g * len(segments) + k) * rows + i * 16
                out[pl.ds(aligned(at), 16), :] = value[:, g * LANES : (g + 1) * LANES]
            return 0

        loop(rows // 16, write, 0)


def add(acc, segments, rows, messages):
    scales = []
    for m in messages:
        head = column_scale(m[pl.ds(0, HEAD), :].astype(jnp.int32).astype(jnp.float32)) * (1.0 / TOP)
        scales.append([jnp.broadcast_to(head[g : g + 1, :], (16, LANES)) for g in range(GROUPS)])
    for k, base in enumerate(segments):
        def step(i, _, base=base, k=k):
            at = pl.ds(aligned(base + i * 16), 16)
            for g in range(GROUPS):
                lanes = pl.ds(g * LANES, LANES)
                value = acc[at, lanes]
                for m, scale in zip(messages, scales):
                    got = m[pl.ds(aligned(HEAD + (g * len(segments) + k) * rows + i * 16), 16), :]
                    value += got.astype(jnp.int32).astype(jnp.float32) * scale[g]
                acc[at, lanes] = value
            return 0

        loop(rows // 16, step, 0)


def kernel(
    left, pattern_left, right, pattern_right, keep, inflated, totals,
    panel, lefts, accs, send1, recv1, send2, recv2, send3, recv3, tsend, trecv,
    lsem, psem, psend, precv, ssem1, rsem1, ssem2, rsem2, ssem3, rsem3, tssem, trsem, late,
):
    core, xyz = place()
    x, y, z = xyz
    col = lax.rem(x, 2)
    pair = (x + 1 - 2 * col, y, z)
    mate = device(1 - core, xyz)
    owner = core == col
    slot = jnp.where(owner, 0, 2)
    fetch = pltpu.make_async_copy(right, panel.at[slot], psem)
    fetch.start()

    def now(part, step):
        return [pick([p[n] for p in PLAN[part]], step) for n in range(3)]

    def load(part, step):
        sub, by, half = now(part, step)
        rows = pl.ds(aligned(START[part] + sub * ROWS[part]), ROWS[part])
        if part == A:
            source = left.at[pl.ds(half * 2, 2), :, lax.rem(x + by, 4) // 2, rows, :]
        elif part == B:
            source = left.at[:, lax.rem(y + by, 4), :, rows, :]
        else:
            source = left.at[lax.rem(z + by, 4), :, :, rows, :]
        return pltpu.make_async_copy(source, lefts[part], lsem.at[part])

    for part in ORDER:
        load(part, jnp.int32(0)).start()

    rounds = (
        [mate] + [device(c, moved(xyz, 1, by)) for by in (1, 2, 3) for c in (core, 1 - core)],
        [device(core, moved(xyz, 0, 2))]
        + [device(core, moved(moved(xyz, 2, by), 0, dx)) for by in (1, 2, 3) for dx in (0, 2)],
    )
    peers = [mate, device(1 - core, pair)] + [device(core, moved(xyz, d, by)) for d in range(3) for by in (1, 3)]
    barrier = pltpu.get_barrier_semaphore()
    for peer in peers:
        pl.semaphore_signal(barrier, inc=1, device_id=peer, device_id_type=MESH)

    fetch.wait()
    for k in range(4):
        for j in range(2):
            at = (slot, pl.ds(k * TILE, TILE), pl.ds(j * TILE, TILE))
            mask = jnp.full((TILE, TILE), pattern_right[j, k].astype(jnp.float32))
            panel[at] = panel[at] * mask.astype(jnp.bfloat16)
    pl.semaphore_wait(barrier, len(peers))

    HALF = DEPTH // 2
    PIECES = 2

    def share():
        return pltpu.make_async_remote_copy(
            panel.at[0], panel.at[0], psend.at[0], precv.at[0], device_id=mate, device_id_type=MESH
        )

    def export(to, piece):
        rows = pl.ds(to * HALF + piece * (HALF // PIECES), HALF // PIECES)
        return pltpu.make_async_remote_copy(
            panel.at[2, rows], panel.at[1, rows], psend.at[1 + to * PIECES + piece], precv.at[1 + piece],
            device_id=device(jnp.int32(to), pair), device_id_type=MESH,
        )

    def forward(piece):
        rows = pl.ds(aligned(core * HALF + piece * (HALF // PIECES)), HALF // PIECES)
        return pltpu.make_async_remote_copy(
            panel.at[1, rows], panel.at[1, rows], psend.at[1 + (2 + piece) + PIECES], precv.at[1 + PIECES + piece],
            device_id=mate, device_id_type=MESH,
        )

    @pl.when(owner)
    def _():
        share().start()

    @pl.when(jnp.logical_not(owner))
    def _():
        for piece in range(PIECES):
            for to in (0, 1):
                export(to, piece).start()
        share().wait_recv()

    def message(ring, part, sub, k):
        send, recv, ssem, rsem = (
            (send1, recv1, ssem1, rsem1),
            (send2, recv2, ssem2, rsem2),
            (send3, recv3, ssem3, rsem3),
        )[ring]
        count, by = (3, k + 1) if ring == 2 else (6, MESSAGES[k][1])
        n = sub * count + k
        return pltpu.make_async_remote_copy(
            send[part].at[n], recv[part].at[n], ssem.at[part, n], rsem.at[part, n],
            device_id=device(core, moved(xyz, RING[part][ring], by)), device_id_type=MESH,
        )

    def base1(part, sub, half):
        return (sub * 2 + half) * (8 * ROWS[part])

    WORK = SUBS * 2 * 8

    def multiply(part, step):
        sub, by, half = now(part, step)
        rows = ROWS[part]
        load(part, step).wait()
        block = lefts[part]
        for a in range(block.shape[0]):
            for b in range(block.shape[1]):
                if part == A:
                    tile = (half * 2 + a) * 8 + b * 2 + lax.rem(x + by, 4) // 2
                elif part == B:
                    tile = a * 8 + lax.rem(y + by, 4) * 2 + b
                else:
                    tile = lax.rem(z + by, 4) * 8 + a * 2 + b
                for k in range(4):
                    at = (a, b, slice(None), pl.ds(k * TILE, TILE))
                    mask = jnp.full((rows, TILE), pattern_left[k, tile].astype(jnp.float32))
                    block[at] = block[at] * mask.astype(jnp.bfloat16)
        columns = lax.rem(by, 2) if part == A else half
        to = jnp.where(by == 0, base1(part, sub, half), WORK * rows)
        accs[part][pl.ds(aligned(to), 8 * rows), :] = jnp.dot(
            block[...].reshape(8 * rows, DEPTH), panel[columns], preferred_element_type=jnp.float32
        )

        @pl.when(step < STEPS - 1)
        def _():
            load(part, step + 1).start()

    def bases2(part, sub, by, half):
        rows = ROWS[part]
        if part == A:
            return [base1(part, sub, half) + (a * 4 + lax.rem(y + by, 4)) * rows for a in (0, 1)]
        if part == B:
            return [base1(part, sub, half) + (lax.rem(z + by, 4) * 2 + b) * rows for b in (0, 1)]
        at = [(half * 2 + a) * 2 + lax.rem(x + by, 4) // 2 for a in (0, 1)]
        return [base1(part, sub, by % 2) + a * rows for a in at]

    def base3(part, sub, by):
        rows = ROWS[part]
        if part == A:
            to = lax.rem(z + by, 4)
            return base1(part, sub, to // 2) + (lax.rem(to, 2) * 4 + y) * rows
        if part == B:
            return base1(part, sub, by % 2) + (z * 2 + lax.rem(x + by, 4) // 2) * rows
        return base1(part, sub, 0) + (lax.rem(y + by, 4) * 2 + x // 2) * rows

    def second_first(sub):
        for part in ORDER:
            for half in (0, 1):
                for k in OWN[half]:
                    message(0, part, sub, k).wait_recv()
                got = [recv1[part].at[sub * 6 + k] for k in OWN[half]]
                add(accs[part], [base1(part, sub, half)], 8 * ROWS[part], got)
            for k in (0, 1, 2, 3):
                encode(accs[part], bases2(part, sub, *MESSAGES[k][0]), ROWS[part], send2[part].at[sub * 6 + k])
                message(1, part, sub, k).start()

    def second_merge(sub):
        for part in ORDER:
            for k, merged in MERGED.items():
                bases = bases2(part, sub, *MESSAGES[k][0])
                message(1, part, sub, merged).wait_recv()
                add(accs[part], bases, ROWS[part], [recv2[part].at[sub * 6 + merged]])
                encode(accs[part], bases, ROWS[part], send2[part].at[sub * 6 + k])
                message(1, part, sub, k).start()

    def third(sub):
        for part in ORDER:
            for half in (0, 1):
                for k in OWN[half]:
                    message(1, part, sub, k).wait_recv()
                got = [recv2[part].at[sub * 6 + k] for k in OWN[half]]
                add(accs[part], bases2(part, sub, 0, half), ROWS[part], got)
            for by in (2, 1, 3):
                encode(accs[part], [base3(part, sub, by)], ROWS[part], send3[part].at[sub * 3 + by - 1])
                message(2, part, sub, by - 1).start()

    keeps = [keep[0, j].astype(jnp.float32) for j in range(2)]
    kept = jnp.concatenate([jnp.full((16, TILE), v) for v in keeps], axis=1)

    def finish(sub, sums):
        for part in ORDER:
            for by in (2, 1, 3):
                message(2, part, sub, by - 1).wait_recv()
            base = base3(part, sub, 0)
            add(accs[part], [base], ROWS[part], [recv3[part].at[sub * 3 + by - 1] for by in (2, 1, 3)])
            for i in range(ROWS[part] // 16):
                value = accs[part][pl.ds(aligned(base + i * 16), 16), :]
                value = value * value * kept
                inflated[pl.ds(START[part] + sub * ROWS[part] + i * 16, 16), :] = value
                sums = sums + value
        return sums

    def steps(step, _):
        @pl.when(step == EARLY)
        def _():
            export(0, 0).wait_recv()
            forward(0).start()

        @pl.when(step == WHOLE)
        def _():
            export(0, 1).wait_recv()
            forward(1).start()

            @pl.when(col == 0)
            def _():
                for sub in range(SUBS):
                    message(0, A, sub, 0).start()

            @pl.when(col == 1)
            def _():
                for sub in range(SUBS):
                    message(0, A, sub, 1).start()

            for piece in range(PIECES):
                forward(piece).wait_recv()

        for part in ORDER:
            rows = 8 * ROWS[part]
            work = WORK * ROWS[part]
            multiply(part, step)
            sub, by, half = now(part, step)

            def is_message(k, by=by, half=half):
                return jnp.logical_and(by == MESSAGES[k][0][0], half == MESSAGES[k][0][1])

            for k, merged in MERGED.items():
                @pl.when(is_message(k))
                def _(merged=merged, part=part, rows=rows, work=work, sub=sub):
                    message(0, part, sub, merged).wait_recv()
                    add(accs[part], [work], rows, [recv1[part].at[sub * 6 + merged]])

            @pl.when(by > 0)
            def _(part=part, rows=rows, work=work, sub=sub):
                k = sum(jnp.where(is_message(n), n, 0) for n in range(6))
                encode(accs[part], [work], rows, send1[part].at[sub * 6 + k])

            for k in range(6):
                ready = is_message(k)
                if part == A and k < 2:
                    ready = jnp.logical_and(ready, col == 1 - k)

                @pl.when(ready)
                def _(k=k, part=part, sub=sub):
                    message(0, part, sub, k).start()

        return 0

    lax.fori_loop(0, STEPS, steps, 0)
    sums = jnp.zeros((16, WIDE), jnp.float32)
    second_first(0)
    pl.semaphore_signal(late, inc=1, device_id=mate, device_id_type=MESH)
    second_first(1)
    second_merge(0)
    second_merge(1)
    third(0)
    third(1)
    sums = finish(0, sums)
    pl.semaphore_wait(late, 1)
    sums = finish(1, sums)
    sums = jnp.sum(sums, axis=0, keepdims=True)

    parts = [sums[:, g * LANES : (g + 1) * LANES] for g in range(GROUPS)]
    total = jnp.concatenate(parts + [jnp.zeros((8 - GROUPS, LANES), jnp.float32)], axis=0)
    copies = []
    for n, group in enumerate(rounds):
        tsend[n] = total
        now = [
            pltpu.make_async_remote_copy(
                tsend.at[n], trecv.at[n, k], tssem.at[n, k], trsem.at[n, k], device_id=peer, device_id_type=MESH
            )
            for k, peer in enumerate(group)
        ]
        for copy in now:
            copy.start()
        for k, copy in enumerate(now):
            copy.wait_recv()
            total = total + trecv[n, k]
        copies += now
    for g in range(GROUPS):
        totals[:, pl.ds(g * LANES, LANES)] = total[g : g + 1, :] + 1e-6

    for copy in copies:
        copy.wait_send()
    for part in range(3):
        for sub in range(SUBS):
            for k in range(6):
                message(0, part, sub, k).wait_send()
                message(1, part, sub, k).wait_send()
            for k in range(3):
                message(2, part, sub, k).wait_send()
    for piece in range(PIECES):
        forward(piece).wait_send()

    @pl.when(owner)
    def _():
        share().wait_send()

    @pl.when(jnp.logical_not(owner))
    def _():
        for piece in range(PIECES):
            for to in (0, 1):
                export(to, piece).wait_send()


def body(left, pattern_left, right, pattern_right, keep):
    vmem = pl.BlockSpec(memory_space=pltpu.VMEM)
    smem = pl.BlockSpec(memory_space=pltpu.SMEM)
    hbm = pl.BlockSpec(memory_space=pl.ANY)
    dma = pltpu.SemaphoreType.DMA
    blocks = [(2, 4), (4, 2), (4, 2)]

    def buffers(count, pieces):
        return [
            pltpu.VMEM((SUBS * count, HEAD + GROUPS * pieces * r, LANES), jnp.int16) for r in ROWS
        ]

    inflated, totals = pl.pallas_call(
        kernel,
        out_shape=(jax.ShapeDtypeStruct((TILE, WIDE), jnp.float32), jax.ShapeDtypeStruct((1, WIDE), jnp.float32)),
        in_specs=[hbm, smem, hbm, smem, smem],
        out_specs=(vmem, vmem),
        scratch_shapes=[
            pltpu.VMEM((3, DEPTH, WIDE), jnp.bfloat16),
            [pltpu.VMEM(b + (r, DEPTH), jnp.bfloat16) for b, r in zip(blocks, ROWS)],
            [pltpu.VMEM(((SUBS * 2 + 1) * 8 * r, WIDE), jnp.float32) for r in ROWS],
            buffers(6, 8), buffers(6, 8), buffers(6, 2), buffers(6, 2), buffers(3, 1), buffers(3, 1),
            pltpu.VMEM((2, 8, LANES), jnp.float32),
            pltpu.VMEM((2, 7, 8, LANES), jnp.float32),
            dma((3,)), dma, dma((7,)), dma((5,)), dma((3, SUBS * 6)), dma((3, SUBS * 6)),
            dma((3, SUBS * 6)), dma((3, SUBS * 6)), dma((3, SUBS * 3)), dma((3, SUBS * 3)), dma((2, 7)), dma((2, 7)),
            pltpu.SemaphoreType.REGULAR,
        ],
        compiler_params=pltpu.CompilerParams(
            collective_id=0, has_side_effects=True, vmem_limit_bytes=60 * 1024 * 1024
        ),
        name="expand",
    )(left.reshape(4, 4, 2, TILE, DEPTH), pattern_left.T, right, pattern_right.T, keep)
    return jnp.float32(16384) * inflated / totals


def solution(mesh):
    return jax.shard_map(
        body,
        mesh=mesh,
        in_specs=(
            P("row", ("layer", "col")),
            P("row", ("layer", "col")),
            P(("layer", "row"), "col"),
            P(("layer", "row"), "col"),
            P(("row", "layer"), "col"),
        ),
        out_specs=P(("row", "layer"), "col"),
        check_vma=False,
    )
```

```python
import math

import jax
import jax.numpy as jnp
from jax import lax
from jax.experimental import pallas as pl
from jax.experimental.pallas import tpu as pltpu
from jax.sharding import PartitionSpec as P

MESH = pl.DeviceIdType.MESH
TILE = 256
DEPTH = 1024
WIDE = 512
LANES = 128
GROUPS = WIDE // LANES
HEAD = 16
FINE = 64
TOP = 32700.0
A, B, C = 0, 1, 2
ORDER = (B, C, A)
LAG = 3
FIRST = ((C, 0), (B, 0), (A, LAG))
SUBS = 2
ROWS = (32, 48, 48)
START = (0, 64, 160)
PLAN_A = (
    (0, 2, 0), (0, 2, 1), (1, 2, 0), (1, 2, 1), (0, 0, 0), (1, 0, 0), (0, 0, 1), (0, 3, 0),
    (0, 1, 1), (0, 1, 0), (0, 3, 1), (1, 3, 0), (1, 1, 1), (1, 1, 0), (1, 3, 1), (1, 0, 1),
)
PLAN_BC = (
    (0, 2, 0), (0, 3, 0), (1, 2, 0), (1, 3, 0), (0, 0, 0), (1, 0, 0), (0, 1, 0), (0, 2, 1),
    (1, 2, 1), (0, 1, 1), (1, 1, 1), (1, 1, 0), (0, 0, 1), (0, 3, 1), (1, 0, 1), (1, 3, 1),
)
PLAN = (PLAN_A, PLAN_BC, PLAN_BC)
STEPS = len(PLAN_A)
EARLY, WHOLE = 5, 7
MESSAGES = (((2, 0), 1), ((2, 1), 3), ((3, 0), 3), ((1, 1), 1), ((1, 0), 1), ((3, 1), 3))
MERGED = {4: 0, 5: 1}
OWN = (2, 4)
RING = ((0, 1, 2), (1, 2, 0), (2, 0, 1))


def place():
    layer = lax.axis_index("layer")
    x = lax.rem(layer, 2) * 2 + lax.axis_index("col")
    return lax.axis_index("row"), (x, lax.rem(layer // 2, 4), layer // 8)


def device(core, xyz):
    x, y, z = xyz
    return (core, lax.rem(x, 2), z * 8 + y * 2 + x // 2)


def moved(xyz, dim, by):
    return tuple(lax.rem(v + by, 4) if d == dim else v for d, v in enumerate(xyz))


def pick(table, index):
    value = jnp.int32(table[-1])
    for k in range(len(table) - 2, -1, -1):
        value = jnp.where(index == k, jnp.int32(table[k]), value)
    return value


def aligned(value, by=16):
    return pl.multiple_of(value, by)


def loop(count, step, init):
    return lax.fori_loop(0, count, step, init, unroll=True if count <= 6 else 4)


def column_scale(codes):
    return jnp.exp(codes * (math.log(2.0) / FINE))


def decoder(sources, rows):
    scales = []
    for m, _, _ in sources:
        head = column_scale(m[pl.ds(0, HEAD), :].astype(jnp.int32).astype(jnp.float32)) * (1.0 / TOP)
        scales.append([jnp.broadcast_to(head[g : g + 1, :], (16, LANES)) for g in range(GROUPS)])

    def read(value, g, k, i):
        for (m, stride, begins), scale in zip(sources, scales):
            got = m[pl.ds(aligned(HEAD + g * stride + begins[k] + i * 16), 16), :]
            value += got.astype(jnp.int32).astype(jnp.float32) * scale[g]
        return value

    return read


def summed(acc, segments, rows, sources, use, init):
    read = decoder(sources, rows)
    for k, base in enumerate(segments):
        def step(i, carry, base=base, k=k):
            at = pl.ds(aligned(base + i * 16), 16)
            if sources:
                groups = [pl.ds(g * LANES, LANES) for g in range(GROUPS)]
                value = jnp.concatenate([read(acc[at, lanes], g, k, i) for g, lanes in enumerate(groups)], axis=1)
            else:
                value = acc[at, :]
            return use(at, value, k, i, carry)

        init = loop(rows // 16, step, init)
    return init


def encode(acc, segments, rows, out, sources=()):
    def look(at, value, k, i, top):
        if sources:
            acc[at, :] = value
        return jnp.maximum(top, jnp.abs(value))

    top = summed(acc, segments, rows, sources, look, jnp.zeros((HEAD, WIDE), jnp.float32))
    top = jnp.max(top, axis=0, keepdims=True)
    codes = jnp.ceil(jnp.log(jnp.maximum(top, 1e-30)) * (FINE / math.log(2.0)))
    row = lax.broadcasted_iota(jnp.int32, (HEAD, LANES), 0)
    head = jnp.zeros((HEAD, LANES), jnp.float32)
    for g in range(GROUPS):
        head = jnp.where(row == g, codes[:, g * LANES : (g + 1) * LANES], head)
    out[pl.ds(0, HEAD), :] = head.astype(jnp.int32).astype(jnp.int16)
    inverse = jnp.broadcast_to(TOP / column_scale(codes), (HEAD, WIDE))

    def write(at, value, k, i, _):
        value = jnp.round(value * inverse).astype(jnp.int32).astype(jnp.int16)
        for g in range(GROUPS):
            to = HEAD + (g * len(segments) + k) * rows + i * 16
            out[pl.ds(aligned(to), 16), :] = value[:, g * LANES : (g + 1) * LANES]
        return 0

    summed(acc, segments, rows, (), write, 0)


def kernel(
    left, pattern_left_in, right, pattern_right_in, keep_in, inflated_out, totals,
    pattern_left, pattern_right, keep, inflated, panel, lefts, accs, send1, recv1, send2, recv2, send3, recv3, tsend, trecv,
    msem, osem, lsem, psem, psend, precv, ssem1, rsem1, ssem2, rsem2, ssem3, rsem3, tssem, trsem, late,
):
    core, xyz = place()
    x, y, z = xyz
    col = lax.rem(x, 2)
    pair = (x + 1 - 2 * col, y, z)
    mate = device(1 - core, xyz)
    owner = core == col
    peers = [mate, device(1 - core, pair)] + [device(core, moved(xyz, d, by)) for d in range(3) for by in (1, 3)]
    barrier = pltpu.get_barrier_semaphore()
    for peer in peers:
        pl.semaphore_signal(barrier, inc=1, device_id=peer, device_id_type=MESH)

    small = [
        pltpu.make_async_copy(pattern_right_in, pattern_right, msem.at[0]),
        pltpu.make_async_copy(pattern_left_in, pattern_left, msem.at[1]),
        pltpu.make_async_copy(keep_in, keep, msem.at[2]),
    ]
    for copy in small:
        copy.start()
    slot = jnp.where(owner, 0, 2)
    fetch = pltpu.make_async_copy(right, panel.at[slot], psem)
    fetch.start()

    def now(part, step):
        return [pick([p[n] for p in PLAN[part]], step) for n in range(3)]

    def load(part, step):
        sub, by, half = now(part, step)
        rows = pl.ds(aligned(START[part] + sub * ROWS[part]), ROWS[part])
        if part == A:
            source = left.at[pl.ds(half * 2, 2), :, lax.rem(x + by, 4) // 2, rows, :]
        elif part == B:
            source = left.at[:, lax.rem(y + by, 4), :, rows, :]
        else:
            source = left.at[lax.rem(z + by, 4), :, :, rows, :]
        return pltpu.make_async_copy(source, lefts[part], lsem.at[part])

    for part in ORDER:
        load(part, jnp.int32(0)).start()

    for copy in small:
        copy.wait()
    fetch.wait()
    for k in range(4):
        for j in range(2):
            at = (slot, pl.ds(k * TILE, TILE), pl.ds(j * TILE, TILE))
            mask = jnp.full((TILE, TILE), pattern_right[j, k].astype(jnp.float32))
            panel[at] = panel[at] * mask.astype(jnp.bfloat16)
    pl.semaphore_wait(barrier, len(peers))

    HALF = DEPTH // 2
    PIECES = 2

    def share():
        return pltpu.make_async_remote_copy(
            panel.at[0], panel.at[0], psend.at[0], precv.at[0], device_id=mate, device_id_type=MESH
        )

    def export(to, piece):
        rows = pl.ds(to * HALF + piece * (HALF // PIECES), HALF // PIECES)
        return pltpu.make_async_remote_copy(
            panel.at[2, rows], panel.at[1, rows], psend.at[1 + to * PIECES + piece], precv.at[1 + piece],
            device_id=device(jnp.int32(to), pair), device_id_type=MESH,
        )

    def forward(piece):
        rows = pl.ds(aligned(core * HALF + piece * (HALF // PIECES)), HALF // PIECES)
        return pltpu.make_async_remote_copy(
            panel.at[1, rows], panel.at[1, rows], psend.at[1 + (2 + piece) + PIECES], precv.at[1 + PIECES + piece],
            device_id=mate, device_id_type=MESH,
        )

    @pl.when(owner)
    def _():
        share().start()

    @pl.when(jnp.logical_not(owner))
    def _():
        for piece in range(PIECES):
            for to in (0, 1):
                export(to, piece).start()
        share().wait_recv()

    def message(ring, part, sub, k):
        send, recv, ssem, rsem = (
            (send1, recv1, ssem1, rsem1),
            (send2, recv2, ssem2, rsem2),
            (send3, recv3, ssem3, rsem3),
        )[ring]
        count, by = (3, k + 1) if ring == 2 else (6, MESSAGES[k][1])
        n = sub * count + k
        return pltpu.make_async_remote_copy(
            send[part].at[n], recv[part].at[n], ssem.at[part, n], rsem.at[part, n],
            device_id=device(core, moved(xyz, RING[part][ring], by)), device_id_type=MESH,
        )

    def base1(part, sub, half):
        return (sub * 2 + half) * (8 * ROWS[part])

    WORK = SUBS * 2 * 8

    def multiply(part, step):
        sub, by, half = now(part, step)
        rows = ROWS[part]
        load(part, step).wait()
        block = lefts[part]
        for a in range(block.shape[0]):
            for b in range(block.shape[1]):
                if part == A:
                    tile = (half * 2 + a) * 8 + b * 2 + lax.rem(x + by, 4) // 2
                elif part == B:
                    tile = a * 8 + lax.rem(y + by, 4) * 2 + b
                else:
                    tile = lax.rem(z + by, 4) * 8 + a * 2 + b
                for k in range(4):
                    at = (a, b, slice(None), pl.ds(k * TILE, TILE))
                    mask = jnp.full((rows, TILE), pattern_left[k, tile].astype(jnp.float32))
                    block[at] = block[at] * mask.astype(jnp.bfloat16)
        columns = lax.rem(by, 2) if part == A else half
        to = jnp.where(by == 0, base1(part, sub, half), WORK * rows)
        accs[part][pl.ds(aligned(to), 8 * rows), :] = jnp.dot(
            block[...].reshape(8 * rows, DEPTH), panel[columns], preferred_element_type=jnp.float32
        )

        @pl.when(step < STEPS - 1)
        def _():
            load(part, step + 1).start()

    def pieces2(part, by, half):
        if part == A:
            return half, [a * 4 + lax.rem(y + by, 4) for a in (0, 1)]
        if part == B:
            return half, [lax.rem(z + by, 4) * 2 + b for b in (0, 1)]
        return by % 2, [(half * 2 + a) * 2 + lax.rem(x + by, 4) // 2 for a in (0, 1)]

    def piece3(part, by):
        if part == A:
            to = lax.rem(z + by, 4)
            return to // 2, lax.rem(to, 2) * 4 + y, to // 2, lax.rem(to, 2)
        if part == B:
            to = lax.rem(x + by, 4) // 2
            return by % 2, z * 2 + to, by % 2, to
        to = lax.rem(y + by, 4)
        return 0, to * 2 + x // 2, to // 2, lax.rem(to, 2)

    def first_sources(part, sub, half, pieces):
        begins = [p * ROWS[part] for p in pieces]
        return [(recv1[part].at[sub * 6 + k + half], 8 * ROWS[part], begins) for k in OWN]

    def second(part, sub, k, sources):
        half, pieces = pieces2(part, *MESSAGES[k][0])
        segments = [base1(part, sub, half) + p * ROWS[part] for p in pieces]
        sources = first_sources(part, sub, half, pieces) + sources
        encode(accs[part], segments, ROWS[part], send2[part].at[sub * 6 + k], sources)
        message(1, part, sub, k).start()

    def second_first(sub):
        for part in ORDER:
            for k in (2, 3, 4, 5):
                message(0, part, sub, k).wait_recv()
            for k in (0, 1):
                second(part, sub, k, [])
        for part in ORDER:
            for k in (2, 3):
                second(part, sub, k, [])

    def second_merge(sub):
        for part in ORDER:
            for k, merged in MERGED.items():
                message(1, part, sub, merged).wait_recv()
                rows = ROWS[part]
                second(part, sub, k, [(recv2[part].at[sub * 6 + merged], 2 * rows, [0, rows])])

    def third_sources(part, sub, by):
        half, piece, half2, place2 = piece3(part, by)
        base = base1(part, sub, half) + piece * ROWS[part]
        sources = first_sources(part, sub, half, [piece])
        sources += [(recv2[part].at[sub * 6 + k + half2], 2 * ROWS[part], [place2 * ROWS[part]]) for k in OWN]
        return base, sources

    def third(sub):
        for part in ORDER:
            for k in (2, 3, 4, 5):
                message(1, part, sub, k).wait_recv()
            for by in (2, 1, 3):
                base, sources = third_sources(part, sub, by)
                encode(accs[part], [base], ROWS[part], send3[part].at[sub * 3 + by - 1], sources)
                message(2, part, sub, by - 1).start()

    keeps = [keep[0, j].astype(jnp.float32) for j in range(2)]
    kept = jnp.concatenate([jnp.full((16, TILE), v) for v in keeps], axis=1)

    def result(part, sub):
        at = pl.ds(START[part] + sub * ROWS[part], ROWS[part])
        return pltpu.make_async_copy(inflated.at[at], inflated_out.at[at], osem.at[part, sub])

    def finish(sub, sums):
        for part in ORDER:
            base, sources = third_sources(part, sub, 0)
            for by in (2, 1, 3):
                message(2, part, sub, by - 1).wait_recv()
                sources.append((recv3[part].at[sub * 3 + by - 1], ROWS[part], [0]))

            def use(at, value, k, i, sums, part=part):
                value = value * value * kept
                inflated[pl.ds(aligned(START[part] + sub * ROWS[part] + i * 16), 16), :] = value
                return sums + value

            sums = summed(accs[part], [base], ROWS[part], sources, use, sums)
            result(part, sub).start()
        return sums

    def turn(part, step):
        rows = 8 * ROWS[part]
        work = WORK * ROWS[part]
        multiply(part, step)
        sub, by, half = now(part, step)

        def is_message(k, by=by, half=half):
            return jnp.logical_and(by == MESSAGES[k][0][0], half == MESSAGES[k][0][1])

        out = sum(jnp.where(is_message(n), n, 0) for n in range(6))
        merges = jnp.logical_or(is_message(4), is_message(5))

        @pl.when(merges)
        def _(part=part, rows=rows, work=work, sub=sub, out=out):
            merged = sub * 6 + jnp.where(out == 4, MERGED[4], MERGED[5])
            for k, m in MERGED.items():
                @pl.when(out == k)
                def _(m=m):
                    message(0, part, sub, m).wait_recv()

            source = (recv1[part].at[merged], rows, [0])
            encode(accs[part], [work], rows, send1[part].at[sub * 6 + out], [source])

        @pl.when(jnp.logical_and(by > 0, jnp.logical_not(merges)))
        def _(part=part, rows=rows, work=work, sub=sub, out=out):
            encode(accs[part], [work], rows, send1[part].at[sub * 6 + out])

        for k in range(6):
            ready = is_message(k)
            if part == A and k < 2:
                ready = jnp.logical_and(ready, col == 1 - k)

            @pl.when(ready)
            def _(k=k, part=part, sub=sub):
                message(0, part, sub, k).start()

    def steps(step, _):
        @pl.when(step == EARLY)
        def _():
            export(0, 0).wait_recv()
            forward(0).start()

        @pl.when(step == WHOLE)
        def _():
            export(0, 1).wait_recv()
            forward(1).start()

            @pl.when(col == 0)
            def _():
                for sub in range(SUBS):
                    message(0, A, sub, 0).start()

            @pl.when(col == 1)
            def _():
                for sub in range(SUBS):
                    message(0, A, sub, 1).start()

            for piece in range(PIECES):
                forward(piece).wait_recv()

        for part, behind in FIRST:
            @pl.when(jnp.logical_and(step >= behind, step < behind + STEPS))
            def _(part=part, behind=behind):
                turn(part, step - behind)

        return 0

    lax.fori_loop(0, STEPS + LAG, steps, 0)
    sums = jnp.zeros((16, WIDE), jnp.float32)
    second_first(0)
    pl.semaphore_signal(late, inc=1, device_id=mate, device_id_type=MESH)
    second_first(1)
    second_merge(0)
    second_merge(1)
    third(0)
    third(1)
    sums = finish(0, sums)
    pl.semaphore_wait(late, 1)
    sums = finish(1, sums)
    sums = jnp.sum(sums, axis=0, keepdims=True)

    rounds = (
        [mate] + [device(c, moved(xyz, 1, by)) for by in (1, 2, 3) for c in (core, 1 - core)],
        [device(core, moved(xyz, 0, 2))]
        + [device(core, moved(moved(xyz, 2, by), 0, dx)) for by in (1, 2, 3) for dx in (0, 2)],
    )
    parts = [sums[:, g * LANES : (g + 1) * LANES] for g in range(GROUPS)]
    total = jnp.concatenate(parts + [jnp.zeros((8 - GROUPS, LANES), jnp.float32)], axis=0)
    copies = []
    for n, group in enumerate(rounds):
        tsend[n] = total
        now = [
            pltpu.make_async_remote_copy(
                tsend.at[n], trecv.at[n, k], tssem.at[n, k], trsem.at[n, k], device_id=peer, device_id_type=MESH
            )
            for k, peer in enumerate(group)
        ]
        for copy in now:
            copy.start()
        for k, copy in enumerate(now):
            copy.wait_recv()
            total = total + trecv[n, k]
        copies += now
    for g in range(GROUPS):
        totals[:, pl.ds(g * LANES, LANES)] = total[g : g + 1, :] + 1e-6

    for copy in copies:
        copy.wait_send()
    for part in range(3):
        for sub in range(SUBS):
            result(part, sub).wait()
            for k in range(6):
                message(0, part, sub, k).wait_send()
                message(1, part, sub, k).wait_send()
            for k in range(3):
                message(2, part, sub, k).wait_send()
    for piece in range(PIECES):
        forward(piece).wait_send()

    @pl.when(owner)
    def _():
        share().wait_send()

    @pl.when(jnp.logical_not(owner))
    def _():
        for piece in range(PIECES):
            for to in (0, 1):
                export(to, piece).wait_send()


def body(left, pattern_left, right, pattern_right, keep):
    vmem = pl.BlockSpec(memory_space=pltpu.VMEM)
    hbm = pl.BlockSpec(memory_space=pl.ANY)
    dma = pltpu.SemaphoreType.DMA
    blocks = [(2, 4), (4, 2), (4, 2)]

    def buffers(count, pieces):
        return [
            pltpu.VMEM((SUBS * count, HEAD + GROUPS * pieces * r, LANES), jnp.int16) for r in ROWS
        ]

    inflated, totals = pl.pallas_call(
        kernel,
        out_shape=(jax.ShapeDtypeStruct((TILE, WIDE), jnp.float32), jax.ShapeDtypeStruct((1, WIDE), jnp.float32)),
        in_specs=[hbm] * 5,
        out_specs=(hbm, vmem),
        scratch_shapes=[
            pltpu.SMEM((4, 32), jnp.int32), pltpu.SMEM((2, 4), jnp.int32), pltpu.SMEM((1, 2), jnp.int32),
            pltpu.VMEM((TILE, WIDE), jnp.float32),
            pltpu.VMEM((3, DEPTH, WIDE), jnp.bfloat16),
            [pltpu.VMEM(b + (r, DEPTH), jnp.bfloat16) for b, r in zip(blocks, ROWS)],
            [pltpu.VMEM(((SUBS * 2 + 1) * 8 * r, WIDE), jnp.float32) for r in ROWS],
            buffers(6, 8), buffers(6, 8), buffers(6, 2), buffers(6, 2), buffers(3, 1), buffers(3, 1),
            pltpu.VMEM((2, 8, LANES), jnp.float32),
            pltpu.VMEM((2, 7, 8, LANES), jnp.float32),
            dma((3,)), dma((3, SUBS)), dma((3,)), dma, dma((7,)), dma((5,)), dma((3, SUBS * 6)), dma((3, SUBS * 6)),
            dma((3, SUBS * 6)), dma((3, SUBS * 6)), dma((3, SUBS * 3)), dma((3, SUBS * 3)), dma((2, 7)), dma((2, 7)),
            pltpu.SemaphoreType.REGULAR,
        ],
        compiler_params=pltpu.CompilerParams(
            collective_id=0, has_side_effects=True, vmem_limit_bytes=60 * 1024 * 1024
        ),
        name="expand",
    )(left.reshape(4, 4, 2, TILE, DEPTH), pattern_left.T, right, pattern_right.T, keep)
    return jnp.float32(16384) * inflated / totals


def solution(mesh):
    return jax.shard_map(
        body,
        mesh=mesh,
        in_specs=(
            P("row", ("layer", "col")),
            P("row", ("layer", "col")),
            P(("layer", "row"), "col"),
            P(("layer", "row"), "col"),
            P(("row", "layer"), "col"),
        ),
        out_specs=P(("row", "layer"), "col"),
        check_vma=False,
    )
```

```python
import math

import jax
import jax.numpy as jnp
from jax import lax
from jax.experimental import pallas as pl
from jax.experimental.pallas import tpu as pltpu
from jax.sharding import PartitionSpec as P

MESH = pl.DeviceIdType.MESH
TILE = 256
DEPTH = 1024
WIDE = 512
LANES = 128
GROUPS = WIDE // LANES
HEAD = 16
FINE = 64
TOP = 32700.0
A, B, C = 0, 1, 2
ORDER = (B, C, A)
LAG = 3
FIRST = ((C, 0), (B, 0), (A, LAG))
SUBS = 2
ROWS = (32, 48, 48)
START = (0, 64, 160)
PLAN_A = (
    (0, 2, 0), (0, 2, 1), (1, 2, 0), (1, 2, 1), (0, 0, 0), (1, 0, 0), (0, 0, 1), (0, 3, 0),
    (0, 1, 1), (0, 1, 0), (0, 3, 1), (1, 3, 0), (1, 1, 1), (1, 1, 0), (1, 3, 1), (1, 0, 1),
)
PLAN_BC = (
    (0, 2, 0), (0, 3, 0), (1, 2, 0), (1, 3, 0), (0, 0, 0), (1, 0, 0), (0, 1, 0), (0, 2, 1),
    (1, 2, 1), (0, 1, 1), (1, 1, 1), (1, 1, 0), (0, 0, 1), (0, 3, 1), (1, 0, 1), (1, 3, 1),
)
PLAN = (PLAN_A, PLAN_BC, PLAN_BC)
STEPS = len(PLAN_A)
EARLY, WHOLE = 5, 7
MESSAGES = (((2, 0), 1), ((2, 1), 3), ((3, 0), 3), ((1, 1), 1), ((1, 0), 1), ((3, 1), 3))
MERGED = {4: 0, 5: 1}
OWN = (2, 4)
RING = (((0, 2, 1), (1, 0, 2), (2, 1, 0)), ((0, 1, 2), (1, 2, 0), (2, 0, 1)))


def place():
    layer = lax.axis_index("layer")
    x = lax.rem(layer, 2) * 2 + lax.axis_index("col")
    return lax.axis_index("row"), (x, lax.rem(layer // 2, 4), layer // 8)


def device(core, xyz):
    x, y, z = xyz
    return (core, lax.rem(x, 2), z * 8 + y * 2 + x // 2)


def moved(xyz, dim, by):
    return tuple(lax.rem(v + by, 4) if d == dim else v for d, v in enumerate(xyz))


def pick(table, index):
    value = jnp.int32(table[-1])
    for k in range(len(table) - 2, -1, -1):
        value = jnp.where(index == k, jnp.int32(table[k]), value)
    return value


def aligned(value, by=16):
    return pl.multiple_of(value, by)


def loop(count, step, init):
    return lax.fori_loop(0, count, step, init, unroll=True if count <= 6 else 4)


def column_scale(codes):
    return jnp.exp(codes * (math.log(2.0) / FINE))


def decoder(sources, rows):
    scales = []
    for m, _, _ in sources:
        head = column_scale(m[pl.ds(0, HEAD), :].astype(jnp.int32).astype(jnp.float32)) * (1.0 / TOP)
        scales.append([jnp.broadcast_to(head[g : g + 1, :], (16, LANES)) for g in range(GROUPS)])

    def read(value, g, k, i):
        for (m, stride, begins), scale in zip(sources, scales):
            got = m[pl.ds(aligned(HEAD + g * stride + begins[k] + i * 16), 16), :]
            value += got.astype(jnp.int32).astype(jnp.float32) * scale[g]
        return value

    return read


def summed(acc, segments, rows, sources, use, init):
    read = decoder(sources, rows)
    for k, base in enumerate(segments):
        def step(i, carry, base=base, k=k):
            at = pl.ds(aligned(base + i * 16), 16)
            if sources:
                groups = [pl.ds(g * LANES, LANES) for g in range(GROUPS)]
                value = jnp.concatenate([read(acc[at, lanes], g, k, i) for g, lanes in enumerate(groups)], axis=1)
            else:
                value = acc[at, :]
            return use(at, value, k, i, carry)

        init = loop(rows // 16, step, init)
    return init


def encode(acc, segments, rows, out, sources=()):
    def look(at, value, k, i, top):
        if sources:
            acc[at, :] = value
        return jnp.maximum(top, jnp.abs(value))

    top = summed(acc, segments, rows, sources, look, jnp.zeros((HEAD, WIDE), jnp.float32))
    top = jnp.max(top, axis=0, keepdims=True)
    codes = jnp.ceil(jnp.log(jnp.maximum(top, 1e-30)) * (FINE / math.log(2.0)))
    row = lax.broadcasted_iota(jnp.int32, (HEAD, LANES), 0)
    head = jnp.zeros((HEAD, LANES), jnp.float32)
    for g in range(GROUPS):
        head = jnp.where(row == g, codes[:, g * LANES : (g + 1) * LANES], head)
    out[pl.ds(0, HEAD), :] = head.astype(jnp.int32).astype(jnp.int16)
    inverse = jnp.broadcast_to(TOP / column_scale(codes), (HEAD, WIDE))

    def write(at, value, k, i, _):
        value = jnp.round(value * inverse).astype(jnp.int32).astype(jnp.int16)
        for g in range(GROUPS):
            to = HEAD + (g * len(segments) + k) * rows + i * 16
            out[pl.ds(aligned(to), 16), :] = value[:, g * LANES : (g + 1) * LANES]
        return 0

    summed(acc, segments, rows, (), write, 0)


def kernel(
    left, pattern_left_in, right, pattern_right_in, keep_in, inflated_out, totals,
    pattern_left, pattern_right, keep, inflated, panel, lefts, accs, send1, recv1, send2, recv2, send3, recv3, tsend, trecv,
    msem, osem, lsem, psem, psend, precv, ssem1, rsem1, ssem2, rsem2, ssem3, rsem3, tssem, trsem, late,
):
    core, xyz = place()
    x, y, z = xyz
    col = lax.rem(x, 2)
    pair = (x + 1 - 2 * col, y, z)
    mate = device(1 - core, xyz)
    owner = core == col
    peers = [mate, device(1 - core, pair)] + [device(core, moved(xyz, d, by)) for d in range(3) for by in (1, 3)]
    barrier = pltpu.get_barrier_semaphore()
    for peer in peers:
        pl.semaphore_signal(barrier, inc=1, device_id=peer, device_id_type=MESH)

    small = [
        pltpu.make_async_copy(pattern_right_in, pattern_right, msem.at[0]),
        pltpu.make_async_copy(pattern_left_in, pattern_left, msem.at[1]),
        pltpu.make_async_copy(keep_in, keep, msem.at[2]),
    ]
    for copy in small:
        copy.start()
    slot = jnp.where(owner, 0, 2)
    fetch = pltpu.make_async_copy(right, panel.at[slot], psem)
    fetch.start()

    def now(part, step):
        return [pick([p[n] for p in PLAN[part]], step) for n in range(3)]

    def load(part, step):
        sub, by, half = now(part, step)
        rows = pl.ds(aligned(START[part] + sub * ROWS[part]), ROWS[part])
        if part == A:
            source = left.at[pl.ds(half * 2, 2), :, lax.rem(x + by, 4) // 2, rows, :]
        elif part == B:
            source = left.at[:, lax.rem(y + by, 4), :, rows, :]
        else:
            source = left.at[lax.rem(z + by, 4), :, :, rows, :]
        return pltpu.make_async_copy(source, lefts[part], lsem.at[part])

    for part in ORDER:
        load(part, jnp.int32(0)).start()

    for copy in small:
        copy.wait()
    fetch.wait()
    for k in range(4):
        for j in range(2):
            at = (slot, pl.ds(k * TILE, TILE), pl.ds(j * TILE, TILE))
            mask = jnp.full((TILE, TILE), pattern_right[j, k].astype(jnp.float32))
            panel[at] = panel[at] * mask.astype(jnp.bfloat16)
    pl.semaphore_wait(barrier, len(peers))

    HALF = DEPTH // 2
    PIECES = 2

    def share():
        return pltpu.make_async_remote_copy(
            panel.at[0], panel.at[0], psend.at[0], precv.at[0], device_id=mate, device_id_type=MESH
        )

    def export(to, piece):
        rows = pl.ds(to * HALF + piece * (HALF // PIECES), HALF // PIECES)
        return pltpu.make_async_remote_copy(
            panel.at[2, rows], panel.at[1, rows], psend.at[1 + to * PIECES + piece], precv.at[1 + piece],
            device_id=device(jnp.int32(to), pair), device_id_type=MESH,
        )

    def forward(piece):
        rows = pl.ds(aligned(core * HALF + piece * (HALF // PIECES)), HALF // PIECES)
        return pltpu.make_async_remote_copy(
            panel.at[1, rows], panel.at[1, rows], psend.at[1 + (2 + piece) + PIECES], precv.at[1 + PIECES + piece],
            device_id=mate, device_id_type=MESH,
        )

    @pl.when(owner)
    def _():
        share().start()

    @pl.when(jnp.logical_not(owner))
    def _():
        for piece in range(PIECES):
            for to in (0, 1):
                export(to, piece).start()
        share().wait_recv()

    def message(ring, part, sub, k):
        send, recv, ssem, rsem = (
            (send1, recv1, ssem1, rsem1),
            (send2, recv2, ssem2, rsem2),
            (send3, recv3, ssem3, rsem3),
        )[ring]
        count, by = (3, k + 1) if ring == 2 else (6, MESSAGES[k][1])
        n = sub * count + k
        return pltpu.make_async_remote_copy(
            send[part].at[n], recv[part].at[n], ssem.at[part, n], rsem.at[part, n],
            device_id=device(core, moved(xyz, RING[sub if ring else 0][part][ring], by)), device_id_type=MESH,
        )

    def base1(part, sub, half):
        return (sub * 2 + half) * (8 * ROWS[part])

    WORK = SUBS * 2 * 8

    def multiply(part, step):
        sub, by, half = now(part, step)
        rows = ROWS[part]
        load(part, step).wait()
        block = lefts[part]
        for a in range(block.shape[0]):
            for b in range(block.shape[1]):
                if part == A:
                    tile = (half * 2 + a) * 8 + b * 2 + lax.rem(x + by, 4) // 2
                elif part == B:
                    tile = a * 8 + lax.rem(y + by, 4) * 2 + b
                else:
                    tile = lax.rem(z + by, 4) * 8 + a * 2 + b
                for k in range(4):
                    at = (a, b, slice(None), pl.ds(k * TILE, TILE))
                    mask = jnp.full((rows, TILE), pattern_left[k, tile].astype(jnp.float32))
                    block[at] = block[at] * mask.astype(jnp.bfloat16)
        columns = lax.rem(by, 2) if part == A else half
        to = jnp.where(by == 0, base1(part, sub, half), WORK * rows)
        accs[part][pl.ds(aligned(to), 8 * rows), :] = jnp.dot(
            block[...].reshape(8 * rows, DEPTH), panel[columns], preferred_element_type=jnp.float32
        )

        @pl.when(step < STEPS - 1)
        def _():
            load(part, step + 1).start()

    def pieces2(part, sub, by, half):
        axis = RING[sub][part][1]
        to = lax.rem(xyz[axis] + by, 4)
        if part == A and axis == 1:
            return half, [a * 4 + to for a in (0, 1)]
        if part == A:
            return to // 2, [lax.rem(to, 2) * 4 + half * 2 + a for a in (0, 1)]
        if axis == 0:
            return by % 2, [(half * 2 + a) * 2 + to // 2 for a in (0, 1)]
        return half, [to * 2 + b for b in (0, 1)]

    def piece3(part, sub, by):
        axis = RING[sub][part][2]
        to = lax.rem(xyz[axis] + by, 4)
        if part == A and axis == 2:
            return to // 2, lax.rem(to, 2) * 4 + y, to // 2, lax.rem(to, 2)
        if part == A:
            return z // 2, lax.rem(z, 2) * 4 + to, to // 2, lax.rem(to, 2)
        if axis == 0:
            return by % 2, xyz[RING[sub][part][1]] * 2 + to // 2, by % 2, to // 2
        return 0, to * 2 + x // 2, to // 2, lax.rem(to, 2)

    def first_sources(part, sub, half, pieces):
        begins = [p * ROWS[part] for p in pieces]
        return [(recv1[part].at[sub * 6 + k + half], 8 * ROWS[part], begins) for k in OWN]

    def second(part, sub, k, sources):
        half, pieces = pieces2(part, sub, *MESSAGES[k][0])
        segments = [base1(part, sub, half) + p * ROWS[part] for p in pieces]
        sources = first_sources(part, sub, half, pieces) + sources
        encode(accs[part], segments, ROWS[part], send2[part].at[sub * 6 + k], sources)
        message(1, part, sub, k).start()

    def second_first(sub):
        for part in ORDER:
            for k in (2, 3, 4, 5):
                message(0, part, sub, k).wait_recv()
            for k in (0, 1):
                second(part, sub, k, [])
        for part in ORDER:
            for k in (2, 3):
                second(part, sub, k, [])

    def second_merge(sub):
        for part in ORDER:
            for k, merged in MERGED.items():
                message(1, part, sub, merged).wait_recv()
                rows = ROWS[part]
                second(part, sub, k, [(recv2[part].at[sub * 6 + merged], 2 * rows, [0, rows])])

    def third_sources(part, sub, by):
        half, piece, half2, place2 = piece3(part, sub, by)
        base = base1(part, sub, half) + piece * ROWS[part]
        sources = first_sources(part, sub, half, [piece])
        sources += [(recv2[part].at[sub * 6 + k + half2], 2 * ROWS[part], [place2 * ROWS[part]]) for k in OWN]
        return base, sources

    def third(sub):
        for part in ORDER:
            for k in (2, 3, 4, 5):
                message(1, part, sub, k).wait_recv()
            for by in (2, 1, 3):
                base, sources = third_sources(part, sub, by)
                encode(accs[part], [base], ROWS[part], send3[part].at[sub * 3 + by - 1], sources)
                message(2, part, sub, by - 1).start()

    keeps = [keep[0, j].astype(jnp.float32) for j in range(2)]
    kept = jnp.concatenate([jnp.full((16, TILE), v) for v in keeps], axis=1)

    def result(part, sub):
        at = pl.ds(START[part] + sub * ROWS[part], ROWS[part])
        return pltpu.make_async_copy(inflated.at[at], inflated_out.at[at], osem.at[part, sub])

    def finish(sub, sums):
        for part in ORDER:
            base, sources = third_sources(part, sub, 0)
            for by in (2, 1, 3):
                message(2, part, sub, by - 1).wait_recv()
                sources.append((recv3[part].at[sub * 3 + by - 1], ROWS[part], [0]))

            def use(at, value, k, i, sums, part=part):
                value = value * value * kept
                inflated[pl.ds(aligned(START[part] + sub * ROWS[part] + i * 16), 16), :] = value
                return sums + value

            sums = summed(accs[part], [base], ROWS[part], sources, use, sums)
            result(part, sub).start()
        return sums

    def turn(part, step):
        rows = 8 * ROWS[part]
        work = WORK * ROWS[part]
        multiply(part, step)
        sub, by, half = now(part, step)

        def is_message(k, by=by, half=half):
            return jnp.logical_and(by == MESSAGES[k][0][0], half == MESSAGES[k][0][1])

        out = sum(jnp.where(is_message(n), n, 0) for n in range(6))
        merges = jnp.logical_or(is_message(4), is_message(5))

        @pl.when(merges)
        def _(part=part, rows=rows, work=work, sub=sub, out=out):
            merged = sub * 6 + jnp.where(out == 4, MERGED[4], MERGED[5])
            for k, m in MERGED.items():
                @pl.when(out == k)
                def _(m=m):
                    message(0, part, sub, m).wait_recv()

            source = (recv1[part].at[merged], rows, [0])
            encode(accs[part], [work], rows, send1[part].at[sub * 6 + out], [source])

        @pl.when(jnp.logical_and(by > 0, jnp.logical_not(merges)))
        def _(part=part, rows=rows, work=work, sub=sub, out=out):
            encode(accs[part], [work], rows, send1[part].at[sub * 6 + out])

        for k in range(6):
            ready = is_message(k)
            if part == A and k < 2:
                ready = jnp.logical_and(ready, col == 1 - k)

            @pl.when(ready)
            def _(k=k, part=part, sub=sub):
                message(0, part, sub, k).start()

    def steps(step, _):
        @pl.when(step == EARLY)
        def _():
            export(0, 0).wait_recv()
            forward(0).start()

        @pl.when(step == WHOLE)
        def _():
            export(0, 1).wait_recv()
            forward(1).start()

            @pl.when(col == 0)
            def _():
                for sub in range(SUBS):
                    message(0, A, sub, 0).start()

            @pl.when(col == 1)
            def _():
                for sub in range(SUBS):
                    message(0, A, sub, 1).start()

            for piece in range(PIECES):
                forward(piece).wait_recv()

        for part, behind in FIRST:
            @pl.when(jnp.logical_and(step >= behind, step < behind + STEPS))
            def _(part=part, behind=behind):
                turn(part, step - behind)

        return 0

    lax.fori_loop(0, STEPS + LAG, steps, 0)
    sums = jnp.zeros((16, WIDE), jnp.float32)
    second_first(0)
    pl.semaphore_signal(late, inc=1, device_id=mate, device_id_type=MESH)
    second_first(1)
    second_merge(0)
    second_merge(1)
    third(0)
    third(1)
    sums = finish(0, sums)
    pl.semaphore_wait(late, 1)
    sums = finish(1, sums)
    sums = jnp.sum(sums, axis=0, keepdims=True)

    rounds = (
        [mate] + [device(c, moved(xyz, 1, by)) for by in (1, 2, 3) for c in (core, 1 - core)],
        [device(core, moved(xyz, 0, 2))]
        + [device(core, moved(moved(xyz, 2, by), 0, dx)) for by in (1, 2, 3) for dx in (0, 2)],
    )
    parts = [sums[:, g * LANES : (g + 1) * LANES] for g in range(GROUPS)]
    total = jnp.concatenate(parts + [jnp.zeros((8 - GROUPS, LANES), jnp.float32)], axis=0)
    copies = []
    for n, group in enumerate(rounds):
        tsend[n] = total
        now = [
            pltpu.make_async_remote_copy(
                tsend.at[n], trecv.at[n, k], tssem.at[n, k], trsem.at[n, k], device_id=peer, device_id_type=MESH
            )
            for k, peer in enumerate(group)
        ]
        for copy in now:
            copy.start()
        for k, copy in enumerate(now):
            copy.wait_recv()
            total = total + trecv[n, k]
        copies += now
    for g in range(GROUPS):
        totals[:, pl.ds(g * LANES, LANES)] = total[g : g + 1, :] + 1e-6

    for copy in copies:
        copy.wait_send()
    for part in range(3):
        for sub in range(SUBS):
            result(part, sub).wait()
            for k in range(6):
                message(0, part, sub, k).wait_send()
                message(1, part, sub, k).wait_send()
            for k in range(3):
                message(2, part, sub, k).wait_send()
    for piece in range(PIECES):
        forward(piece).wait_send()

    @pl.when(owner)
    def _():
        share().wait_send()

    @pl.when(jnp.logical_not(owner))
    def _():
        for piece in range(PIECES):
            for to in (0, 1):
                export(to, piece).wait_send()


def body(left, pattern_left, right, pattern_right, keep):
    vmem = pl.BlockSpec(memory_space=pltpu.VMEM)
    hbm = pl.BlockSpec(memory_space=pl.ANY)
    dma = pltpu.SemaphoreType.DMA
    blocks = [(2, 4), (4, 2), (4, 2)]

    def buffers(count, pieces):
        return [
            pltpu.VMEM((SUBS * count, HEAD + GROUPS * pieces * r, LANES), jnp.int16) for r in ROWS
        ]

    inflated, totals = pl.pallas_call(
        kernel,
        out_shape=(jax.ShapeDtypeStruct((TILE, WIDE), jnp.float32), jax.ShapeDtypeStruct((1, WIDE), jnp.float32)),
        in_specs=[hbm] * 5,
        out_specs=(hbm, vmem),
        scratch_shapes=[
            pltpu.SMEM((4, 32), jnp.int32), pltpu.SMEM((2, 4), jnp.int32), pltpu.SMEM((1, 2), jnp.int32),
            pltpu.VMEM((TILE, WIDE), jnp.float32),
            pltpu.VMEM((3, DEPTH, WIDE), jnp.bfloat16),
            [pltpu.VMEM(b + (r, DEPTH), jnp.bfloat16) for b, r in zip(blocks, ROWS)],
            [pltpu.VMEM(((SUBS * 2 + 1) * 8 * r, WIDE), jnp.float32) for r in ROWS],
            buffers(6, 8), buffers(6, 8), buffers(6, 2), buffers(6, 2), buffers(3, 1), buffers(3, 1),
            pltpu.VMEM((2, 8, LANES), jnp.float32),
            pltpu.VMEM((2, 7, 8, LANES), jnp.float32),
            dma((3,)), dma((3, SUBS)), dma((3,)), dma, dma((7,)), dma((5,)), dma((3, SUBS * 6)), dma((3, SUBS * 6)),
            dma((3, SUBS * 6)), dma((3, SUBS * 6)), dma((3, SUBS * 3)), dma((3, SUBS * 3)), dma((2, 7)), dma((2, 7)),
            pltpu.SemaphoreType.REGULAR,
        ],
        compiler_params=pltpu.CompilerParams(
            collective_id=0, has_side_effects=True, vmem_limit_bytes=60 * 1024 * 1024
        ),
        name="expand",
    )(left.reshape(4, 4, 2, TILE, DEPTH), pattern_left.T, right, pattern_right.T, keep)
    return jnp.float32(16384) * inflated / totals


def solution(mesh):
    return jax.shard_map(
        body,
        mesh=mesh,
        in_specs=(
            P("row", ("layer", "col")),
            P("row", ("layer", "col")),
            P(("layer", "row"), "col"),
            P(("layer", "row"), "col"),
            P(("row", "layer"), "col"),
        ),
        out_specs=P(("row", "layer"), "col"),
        check_vma=False,
    )
```

```python
import math

import jax
import jax.numpy as jnp
from jax import lax
from jax.experimental import pallas as pl
from jax.experimental.pallas import tpu as pltpu
from jax.sharding import PartitionSpec as P

MESH = pl.DeviceIdType.MESH
TILE = 256
DEPTH = 1024
WIDE = 512
LANES = 128
GROUPS = WIDE // LANES
HEAD = 16
FINE = 64
TOP = 32700.0
A, B, C = 0, 1, 2
ORDER = (B, C, A)
LAG = 3
FIRST = ((C, 0), (B, 0), (A, LAG))
SUBS = 2
ROWS = (32, 48, 48)
START = (0, 64, 160)
PLAN_A = (
    (0, 2, 0), (0, 2, 1), (1, 2, 0), (1, 2, 1), (0, 0, 0), (1, 0, 0), (0, 0, 1), (0, 3, 0),
    (0, 1, 1), (0, 1, 0), (0, 3, 1), (1, 3, 0), (1, 1, 1), (1, 1, 0), (1, 3, 1), (1, 0, 1),
)
PLAN_BC = (
    (0, 2, 0), (0, 3, 0), (1, 2, 0), (1, 3, 0), (0, 0, 0), (1, 0, 0), (0, 1, 0), (0, 2, 1),
    (1, 2, 1), (0, 1, 1), (1, 1, 1), (1, 1, 0), (0, 0, 1), (0, 3, 1), (1, 0, 1), (1, 3, 1),
)
PLAN = (PLAN_A, PLAN_BC, PLAN_BC)
STEPS = len(PLAN_A)
EARLY, WHOLE = 5, 7
MESSAGES = (((2, 0), 1), ((2, 1), 3), ((3, 0), 3), ((1, 1), 1), ((1, 0), 1), ((3, 1), 3))
MERGED = {4: 0, 5: 1}
OWN = (2, 4)
RING = (((0, 2, 1), (1, 0, 2), (2, 1, 0)), ((0, 1, 2), (1, 2, 0), (2, 0, 1)))


def place():
    layer = lax.axis_index("layer")
    x = lax.rem(layer, 2) * 2 + lax.axis_index("col")
    return lax.axis_index("row"), (x, lax.rem(layer // 2, 4), layer // 8)


def device(core, xyz):
    x, y, z = xyz
    return (core, lax.rem(x, 2), z * 8 + y * 2 + x // 2)


def moved(xyz, dim, by):
    return tuple(lax.rem(v + by, 4) if d == dim else v for d, v in enumerate(xyz))


def pick(table, index):
    value = jnp.int32(table[-1])
    for k in range(len(table) - 2, -1, -1):
        value = jnp.where(index == k, jnp.int32(table[k]), value)
    return value


def aligned(value, by=16):
    return pl.multiple_of(value, by)


def loop(count, step, init):
    return lax.fori_loop(0, count, step, init, unroll=True if count <= 6 else 8)


def column_scale(codes):
    return jnp.exp(codes * (math.log(2.0) / FINE))


def decoder(sources, rows):
    scales = []
    for m, _, _ in sources:
        head = column_scale(m[pl.ds(0, HEAD), :].astype(jnp.int32).astype(jnp.float32)) * (1.0 / TOP)
        scales.append([jnp.broadcast_to(head[g : g + 1, :], (16, LANES)) for g in range(GROUPS)])

    def read(value, g, k, i):
        for (m, stride, begins), scale in zip(sources, scales):
            got = m[pl.ds(aligned(HEAD + g * stride + begins[k] + i * 16), 16), :]
            value += got.astype(jnp.int32).astype(jnp.float32) * scale[g]
        return value

    return read


def summed(acc, segments, rows, sources, use, init):
    read = decoder(sources, rows)
    for k, base in enumerate(segments):
        def step(i, carry, base=base, k=k):
            at = pl.ds(aligned(base + i * 16), 16)
            if sources:
                groups = [pl.ds(g * LANES, LANES) for g in range(GROUPS)]
                value = jnp.concatenate([read(acc[at, lanes], g, k, i) for g, lanes in enumerate(groups)], axis=1)
            else:
                value = acc[at, :]
            return use(at, value, k, i, carry)

        init = loop(rows // 16, step, init)
    return init


def encode(acc, segments, rows, out, sources=()):
    def look(at, value, k, i, top):
        if sources:
            acc[at, :] = value
        return jnp.maximum(top, jnp.abs(value))

    top = summed(acc, segments, rows, sources, look, jnp.zeros((HEAD, WIDE), jnp.float32))
    top = jnp.max(top, axis=0, keepdims=True)
    codes = jnp.ceil(jnp.log(jnp.maximum(top, 1e-30)) * (FINE / math.log(2.0)))
    row = lax.broadcasted_iota(jnp.int32, (HEAD, LANES), 0)
    head = jnp.zeros((HEAD, LANES), jnp.float32)
    for g in range(GROUPS):
        head = jnp.where(row == g, codes[:, g * LANES : (g + 1) * LANES], head)
    out[pl.ds(0, HEAD), :] = head.astype(jnp.int32).astype(jnp.int16)
    inverse = jnp.broadcast_to(TOP / column_scale(codes), (HEAD, WIDE))

    def write(at, value, k, i, _):
        value = jnp.round(value * inverse).astype(jnp.int32).astype(jnp.int16)
        for g in range(GROUPS):
            to = HEAD + (g * len(segments) + k) * rows + i * 16
            out[pl.ds(aligned(to), 16), :] = value[:, g * LANES : (g + 1) * LANES]
        return 0

    summed(acc, segments, rows, (), write, 0)


def kernel(
    left, pattern_left_in, right, pattern_right_in, keep_in, inflated_out, totals,
    pattern_left, pattern_right, keep, inflated, panel, lefts, accs, send1, recv1, send2, recv2, send3, recv3, tsend, trecv,
    msem, osem, lsem, psem, psend, precv, ssem1, rsem1, ssem2, rsem2, ssem3, rsem3, tssem, trsem, late,
):
    core, xyz = place()
    x, y, z = xyz
    col = lax.rem(x, 2)
    pair = (x + 1 - 2 * col, y, z)
    mate = device(1 - core, xyz)
    owner = core == col
    peers = [device(1 - core, pair)] + [device(core, moved(xyz, d, by)) for d in range(3) for by in (1, 3)] + [mate]
    barrier = pltpu.get_barrier_semaphore()
    for peer in peers:
        pl.semaphore_signal(barrier, inc=1, device_id=peer, device_id_type=MESH)

    slot = jnp.where(owner, 0, 2)
    fetch = pltpu.make_async_copy(right, panel.at[slot], psem)
    fetch.start()

    small = [
        pltpu.make_async_copy(pattern_right_in, pattern_right, msem.at[0]),
        pltpu.make_async_copy(pattern_left_in, pattern_left, msem.at[1]),
        pltpu.make_async_copy(keep_in, keep, msem.at[2]),
    ]
    for copy in small:
        copy.start()
    def now(part, step):
        return [pick([p[n] for p in PLAN[part]], step) for n in range(3)]

    def load(part, step):
        sub, by, half = now(part, step)
        rows = pl.ds(aligned(START[part] + sub * ROWS[part]), ROWS[part])
        if part == A:
            source = left.at[pl.ds(half * 2, 2), :, lax.rem(x + by, 4) // 2, rows, :]
        elif part == B:
            source = left.at[:, lax.rem(y + by, 4), :, rows, :]
        else:
            source = left.at[lax.rem(z + by, 4), :, :, rows, :]
        return pltpu.make_async_copy(source, lefts[part], lsem.at[part])

    for part in ORDER:
        load(part, jnp.int32(0)).start()

    for copy in small:
        copy.wait()
    fetch.wait()
    for k in range(4):
        for j in range(2):
            at = (slot, pl.ds(k * TILE, TILE), pl.ds(j * TILE, TILE))
            mask = jnp.full((TILE, TILE), pattern_right[j, k].astype(jnp.float32))
            panel[at] = panel[at] * mask.astype(jnp.bfloat16)
    pl.semaphore_wait(barrier, len(peers))

    HALF = DEPTH // 2
    PIECES = 2

    def share():
        return pltpu.make_async_remote_copy(
            panel.at[0], panel.at[0], psend.at[0], precv.at[0], device_id=mate, device_id_type=MESH
        )

    def export(to, piece):
        rows = pl.ds(to * HALF + piece * (HALF // PIECES), HALF // PIECES)
        return pltpu.make_async_remote_copy(
            panel.at[2, rows], panel.at[1, rows], psend.at[1 + to * PIECES + piece], precv.at[1 + piece],
            device_id=device(jnp.int32(to), pair), device_id_type=MESH,
        )

    def forward(piece):
        rows = pl.ds(aligned(core * HALF + piece * (HALF // PIECES)), HALF // PIECES)
        return pltpu.make_async_remote_copy(
            panel.at[1, rows], panel.at[1, rows], psend.at[1 + (2 + piece) + PIECES], precv.at[1 + PIECES + piece],
            device_id=mate, device_id_type=MESH,
        )

    @pl.when(owner)
    def _():
        share().start()

    @pl.when(jnp.logical_not(owner))
    def _():
        for piece in range(PIECES):
            for to in (0, 1):
                export(to, piece).start()
        share().wait_recv()

    def message(ring, part, sub, k):
        send, recv, ssem, rsem = (
            (send1, recv1, ssem1, rsem1),
            (send2, recv2, ssem2, rsem2),
            (send3, recv3, ssem3, rsem3),
        )[ring]
        count, by = (3, k + 1) if ring == 2 else (6, MESSAGES[k][1])
        n = sub * count + k
        return pltpu.make_async_remote_copy(
            send[part].at[n], recv[part].at[n], ssem.at[part, n], rsem.at[part, n],
            device_id=device(core, moved(xyz, RING[sub if ring else 0][part][ring], by)), device_id_type=MESH,
        )

    def base1(part, sub, half):
        return (sub * 2 + half) * (8 * ROWS[part])

    WORK = SUBS * 2 * 8

    def multiply(part, step):
        sub, by, half = now(part, step)
        rows = ROWS[part]
        load(part, step).wait()
        block = lefts[part]
        for a in range(block.shape[0]):
            for b in range(block.shape[1]):
                if part == A:
                    tile = (half * 2 + a) * 8 + b * 2 + lax.rem(x + by, 4) // 2
                elif part == B:
                    tile = a * 8 + lax.rem(y + by, 4) * 2 + b
                else:
                    tile = lax.rem(z + by, 4) * 8 + a * 2 + b
                for k in range(4):
                    at = (a, b, slice(None), pl.ds(k * TILE, TILE))
                    mask = jnp.full((rows, TILE), pattern_left[k, tile].astype(jnp.float32))
                    block[at] = block[at] * mask.astype(jnp.bfloat16)
        columns = lax.rem(by, 2) if part == A else half
        to = jnp.where(by == 0, base1(part, sub, half), WORK * rows)
        accs[part][pl.ds(aligned(to), 8 * rows), :] = jnp.dot(
            block[...].reshape(8 * rows, DEPTH), panel[columns], preferred_element_type=jnp.float32
        )

        @pl.when(step < STEPS - 1)
        def _():
            load(part, step + 1).start()

    def pieces2(part, sub, by, half):
        axis = RING[sub][part][1]
        to = lax.rem(xyz[axis] + by, 4)
        if part == A and axis == 1:
            return half, [a * 4 + to for a in (0, 1)]
        if part == A:
            return to // 2, [lax.rem(to, 2) * 4 + half * 2 + a for a in (0, 1)]
        if axis == 0:
            return by % 2, [(half * 2 + a) * 2 + to // 2 for a in (0, 1)]
        return half, [to * 2 + b for b in (0, 1)]

    def piece3(part, sub, by):
        axis = RING[sub][part][2]
        to = lax.rem(xyz[axis] + by, 4)
        if part == A and axis == 2:
            return to // 2, lax.rem(to, 2) * 4 + y, to // 2, lax.rem(to, 2)
        if part == A:
            return z // 2, lax.rem(z, 2) * 4 + to, to // 2, lax.rem(to, 2)
        if axis == 0:
            return by % 2, xyz[RING[sub][part][1]] * 2 + to // 2, by % 2, to // 2
        return 0, to * 2 + x // 2, to // 2, lax.rem(to, 2)

    def first_sources(part, sub, half, pieces):
        begins = [p * ROWS[part] for p in pieces]
        return [(recv1[part].at[sub * 6 + k + half], 8 * ROWS[part], begins) for k in OWN]

    def second(part, sub, k, sources):
        half, pieces = pieces2(part, sub, *MESSAGES[k][0])
        segments = [base1(part, sub, half) + p * ROWS[part] for p in pieces]
        sources = first_sources(part, sub, half, pieces) + sources
        encode(accs[part], segments, ROWS[part], send2[part].at[sub * 6 + k], sources)
        message(1, part, sub, k).start()

    def second_first(sub):
        for part in ORDER:
            for k in (2, 3, 4, 5):
                message(0, part, sub, k).wait_recv()
            for k in (0, 1):
                second(part, sub, k, [])
        for part in ORDER:
            for k in (2, 3):
                second(part, sub, k, [])

    def second_merge(sub):
        for part in ORDER:
            for k, merged in MERGED.items():
                message(1, part, sub, merged).wait_recv()
                rows = ROWS[part]
                second(part, sub, k, [(recv2[part].at[sub * 6 + merged], 2 * rows, [0, rows])])

    def third_sources(part, sub, by):
        half, piece, half2, place2 = piece3(part, sub, by)
        base = base1(part, sub, half) + piece * ROWS[part]
        sources = first_sources(part, sub, half, [piece])
        sources += [(recv2[part].at[sub * 6 + k + half2], 2 * ROWS[part], [place2 * ROWS[part]]) for k in OWN]
        return base, sources

    def third(sub):
        for part in ORDER:
            for k in (2, 3, 4, 5):
                message(1, part, sub, k).wait_recv()
            for by in (2, 1, 3):
                base, sources = third_sources(part, sub, by)
                encode(accs[part], [base], ROWS[part], send3[part].at[sub * 3 + by - 1], sources)
                message(2, part, sub, by - 1).start()

    keeps = [keep[0, j].astype(jnp.float32) for j in range(2)]
    kept = jnp.concatenate([jnp.full((16, TILE), v) for v in keeps], axis=1)

    def result(part, sub):
        at = pl.ds(START[part] + sub * ROWS[part], ROWS[part])
        return pltpu.make_async_copy(inflated.at[at], inflated_out.at[at], osem.at[part, sub])

    def finish(sub, sums):
        for part in ORDER:
            base, sources = third_sources(part, sub, 0)
            for by in (2, 1, 3):
                message(2, part, sub, by - 1).wait_recv()
                sources.append((recv3[part].at[sub * 3 + by - 1], ROWS[part], [0]))

            def use(at, value, k, i, sums, part=part):
                value = value * value * kept
                inflated[pl.ds(aligned(START[part] + sub * ROWS[part] + i * 16), 16), :] = value
                return sums + value

            sums = summed(accs[part], [base], ROWS[part], sources, use, sums)
            result(part, sub).start()
        return sums

    def turn(part, step):
        rows = 8 * ROWS[part]
        work = WORK * ROWS[part]
        multiply(part, step)
        sub, by, half = now(part, step)

        def is_message(k, by=by, half=half):
            return jnp.logical_and(by == MESSAGES[k][0][0], half == MESSAGES[k][0][1])

        out = sum(jnp.where(is_message(n), n, 0) for n in range(6))
        merges = jnp.logical_or(is_message(4), is_message(5))

        @pl.when(merges)
        def _(part=part, rows=rows, work=work, sub=sub, out=out):
            merged = sub * 6 + jnp.where(out == 4, MERGED[4], MERGED[5])
            for k, m in MERGED.items():
                @pl.when(out == k)
                def _(m=m):
                    message(0, part, sub, m).wait_recv()

            source = (recv1[part].at[merged], rows, [0])
            encode(accs[part], [work], rows, send1[part].at[sub * 6 + out], [source])

        @pl.when(jnp.logical_and(by > 0, jnp.logical_not(merges)))
        def _(part=part, rows=rows, work=work, sub=sub, out=out):
            encode(accs[part], [work], rows, send1[part].at[sub * 6 + out])

        for k in range(6):
            ready = is_message(k)
            if part == A and k < 2:
                ready = jnp.logical_and(ready, col == 1 - k)

            @pl.when(ready)
            def _(k=k, part=part, sub=sub):
                message(0, part, sub, k).start()

    def steps(step, _):
        @pl.when(step == EARLY)
        def _():
            export(0, 0).wait_recv()
            forward(0).start()

        @pl.when(step == WHOLE)
        def _():
            export(0, 1).wait_recv()
            forward(1).start()

            @pl.when(col == 0)
            def _():
                for sub in range(SUBS):
                    message(0, A, sub, 0).start()

            @pl.when(col == 1)
            def _():
                for sub in range(SUBS):
                    message(0, A, sub, 1).start()

            for piece in range(PIECES):
                forward(piece).wait_recv()

        for part, behind in FIRST:
            @pl.when(jnp.logical_and(step >= behind, step < behind + STEPS))
            def _(part=part, behind=behind):
                turn(part, step - behind)

        return 0

    lax.fori_loop(0, STEPS + LAG, steps, 0)
    sums = jnp.zeros((16, WIDE), jnp.float32)
    second_first(0)
    pl.semaphore_signal(late, inc=1, device_id=mate, device_id_type=MESH)
    second_first(1)
    second_merge(0)
    second_merge(1)
    third(0)
    third(1)
    sums = finish(0, sums)
    pl.semaphore_wait(late, 1)
    sums = finish(1, sums)
    sums = jnp.sum(sums, axis=0, keepdims=True)

    rounds = (
        [mate] + [device(c, moved(xyz, 1, by)) for by in (1, 2, 3) for c in (core, 1 - core)],
        [device(core, moved(xyz, 0, 2))]
        + [device(core, moved(moved(xyz, 2, by), 0, dx)) for by in (1, 2, 3) for dx in (0, 2)],
    )
    parts = [sums[:, g * LANES : (g + 1) * LANES] for g in range(GROUPS)]
    total = jnp.concatenate(parts + [jnp.zeros((8 - GROUPS, LANES), jnp.float32)], axis=0)
    copies = []
    for n, group in enumerate(rounds):
        tsend[n] = total
        now = [
            pltpu.make_async_remote_copy(
                tsend.at[n], trecv.at[n, k], tssem.at[n, k], trsem.at[n, k], device_id=peer, device_id_type=MESH
            )
            for k, peer in enumerate(group)
        ]
        for copy in now:
            copy.start()
        for k, copy in enumerate(now):
            copy.wait_recv()
            total = total + trecv[n, k]
        copies += now
    for g in range(GROUPS):
        totals[:, pl.ds(g * LANES, LANES)] = total[g : g + 1, :] + 1e-6

    for copy in copies:
        copy.wait_send()
    for part in range(3):
        for sub in range(SUBS):
            result(part, sub).wait()
            for k in range(6):
                message(0, part, sub, k).wait_send()
                message(1, part, sub, k).wait_send()
            for k in range(3):
                message(2, part, sub, k).wait_send()
    for piece in range(PIECES):
        forward(piece).wait_send()

    @pl.when(owner)
    def _():
        share().wait_send()

    @pl.when(jnp.logical_not(owner))
    def _():
        for piece in range(PIECES):
            for to in (0, 1):
                export(to, piece).wait_send()


def body(left, pattern_left, right, pattern_right, keep):
    vmem = pl.BlockSpec(memory_space=pltpu.VMEM)
    hbm = pl.BlockSpec(memory_space=pl.ANY)
    dma = pltpu.SemaphoreType.DMA
    blocks = [(2, 4), (4, 2), (4, 2)]

    def buffers(count, pieces):
        return [
            pltpu.VMEM((SUBS * count, HEAD + GROUPS * pieces * r, LANES), jnp.int16) for r in ROWS
        ]

    inflated, totals = pl.pallas_call(
        kernel,
        out_shape=(jax.ShapeDtypeStruct((TILE, WIDE), jnp.float32), jax.ShapeDtypeStruct((1, WIDE), jnp.float32)),
        in_specs=[hbm] * 5,
        out_specs=(hbm, vmem),
        scratch_shapes=[
            pltpu.SMEM((4, 32), jnp.int32), pltpu.SMEM((2, 4), jnp.int32), pltpu.SMEM((1, 2), jnp.int32),
            pltpu.VMEM((TILE, WIDE), jnp.float32),
            pltpu.VMEM((3, DEPTH, WIDE), jnp.bfloat16),
            [pltpu.VMEM(b + (r, DEPTH), jnp.bfloat16) for b, r in zip(blocks, ROWS)],
            [pltpu.VMEM(((SUBS * 2 + 1) * 8 * r, WIDE), jnp.float32) for r in ROWS],
            buffers(6, 8), buffers(6, 8), buffers(6, 2), buffers(6, 2), buffers(3, 1), buffers(3, 1),
            pltpu.VMEM((2, 8, LANES), jnp.float32),
            pltpu.VMEM((2, 7, 8, LANES), jnp.float32),
            dma((3,)), dma((3, SUBS)), dma((3,)), dma, dma((7,)), dma((5,)), dma((3, SUBS * 6)), dma((3, SUBS * 6)),
            dma((3, SUBS * 6)), dma((3, SUBS * 6)), dma((3, SUBS * 3)), dma((3, SUBS * 3)), dma((2, 7)), dma((2, 7)),
            pltpu.SemaphoreType.REGULAR,
        ],
        compiler_params=pltpu.CompilerParams(
            collective_id=0, has_side_effects=True, vmem_limit_bytes=60 * 1024 * 1024
        ),
        name="expand",
    )(left.reshape(4, 4, 2, TILE, DEPTH), pattern_left.T, right, pattern_right.T, keep)
    return jnp.float32(16384) * inflated / totals


def solution(mesh):
    return jax.shard_map(
        body,
        mesh=mesh,
        in_specs=(
            P("row", ("layer", "col")),
            P("row", ("layer", "col")),
            P(("layer", "row"), "col"),
            P(("layer", "row"), "col"),
            P(("row", "layer"), "col"),
        ),
        out_specs=P(("row", "layer"), "col"),
        check_vma=False,
    )
```
